32 devices in a mesh: date: 4 (over y, x), az: 8 (over z, core).
Axes of the slice: x: 2, y: 2, z: 4, core: 2. Of those that a mesh axis runs over, the one named last changes fastest.
Arguments:
- epoch_image_tensor: bfloat16 [16, 2, 2560, 1280], P('date', None, 'az'), may hold values from -5 to 5
- along_track_shifts: int32 [16, 40, 20], P('date', 'az'), may hold values from -32 to 32, as said below
- cross_track_shifts: int32 [16, 40, 20], P('date', 'az'), may hold values from -32 to 32, as said below
- epoch_present_table: int32 [16, 40], P('date', 'az'), may hold values 0 or 1
Outputs:
- tile_similarity: float32 [16, 40, 20], P('date', 'az')
- smoothed_ifgs: float32 [16, 2, 512, 64], P('date', None, 'az')
The draws below stay inside these ranges and needn't reach their ends.
Inputs may be any that keep to these rules, and one draw needn't show every extreme that they name: `along_track_shifts`: date 0 has all offsets zero. `cross_track_shifts`: date 0 has all offsets zero.
All inputs are finite; a program needn't handle non-finite values. Where the reference program divides by a largest or mean magnitude, that divisor is 1e-20 or more. No bound on the sum of `epoch_present_table` on one device may be relied on, other than what follows from the above.
Results may differ from the reference program's by a relative error of at most 0.0003.
Values may be sent and summed in bfloat16 or wider, within the bound.
A program may use at most 192 MiB of HBM per device.

```python
import jax
import jax.numpy as jnp
from jax import lax

RG = 1280
WIN = 64
MARGIN_LINES = 32
RHALO = 32
LOOK_AZ = 5
LOOK_RG = 20
PATCH = 32
EPOCH_COUNT = 16
AZ = 2560
TILES_ALONG = 40
MA = 512
MR = 64


def shift_fields(key):
    tensor_extent = (EPOCH_COUNT, AZ // WIN, RG // WIN)
    shift_rows = jax.random.randint(jax.random.fold_in(key, 11), tensor_extent, -MARGIN_LINES, MARGIN_LINES + 1)
    shift_cols = jax.random.randint(jax.random.fold_in(key, 12), tensor_extent, -RHALO, RHALO + 1)
    later = (jnp.arange(EPOCH_COUNT) > 0).astype(jnp.int32)[:, None, None]
    return ((shift_rows * later).astype(jnp.int32), (shift_cols * later).astype(jnp.int32))


def draw_along_track_shifts(key, part):
    return shift_fields(key)[0]


def draw_cross_track_shifts(key, part):
    return shift_fields(key)[1]


def draw_epoch_image_tensor(key, part):
    shift_rows, shift_cols = shift_fields(key)
    common = jax.random.normal(jax.random.fold_in(key, 21), (2, AZ, RG), jnp.float32)
    line_index = jnp.arange(AZ)[:, None]
    sample_index = jnp.arange(RG)[None, :]

    def lone_epoch(date_index):
        along_rows = shift_rows[date_index][line_index // WIN, sample_index // WIN]
        along_cols = shift_cols[date_index][line_index // WIN, sample_index // WIN]
        source_rows = jnp.clip(line_index - along_rows, 0, AZ - 1)
        source_cols = jnp.clip(sample_index - along_cols, 0, RG - 1)
        moved = common[:, source_rows, source_cols]
        noise = jax.random.normal(jax.random.fold_in(jax.random.fold_in(key, 23), date_index), (2, AZ, RG), jnp.float32)
        return jnp.clip(0.8 * moved + 0.6 * noise, -5.0, 5.0).astype(jnp.bfloat16)
    return lax.map(lone_epoch, jnp.arange(EPOCH_COUNT))


def with_ends(values, rng, smallest, high):
    longest = values.shape.index(max(values.shape))
    spots = []
    for shift in (0, 1):
        where = [jax.random.randint(jax.random.fold_in(rng, axis), (), 0, length) for axis, length in enumerate(values.shape)]
        where[longest] = (where[longest] + shift) % values.shape[longest]
        spots.append(tuple(where))
    return values.at[spots[0]].set(smallest).at[spots[1]].set(high)


def setup_inputs(seed: int = 0) -> dict:
    key_list = jax.random.split(jax.random.key(seed), 5)
    epoch_image_tensor = draw_epoch_image_tensor(jax.random.fold_in(key_list[4], 71), 0)
    along_track_shifts = draw_along_track_shifts(jax.random.fold_in(key_list[4], 71), 0)
    cross_track_shifts = draw_cross_track_shifts(jax.random.fold_in(key_list[4], 71), 0)
    epoch_present_table = with_ends((jax.random.randint(key_list[3], (EPOCH_COUNT, TILES_ALONG), 0, 8) < 7).astype(jnp.int32), jax.random.fold_in(key_list[3], 1), 0, 1)
    return {"epoch_image_tensor": epoch_image_tensor, "along_track_shifts": along_track_shifts, "cross_track_shifts": cross_track_shifts, "epoch_present_table": epoch_present_table}


VAR_EPS = 1e-05
RMS_EPS = 1e-06

def goldstein(looks):
    complex_looks = looks[0] + 1j * looks[1]
    patches = complex_looks.reshape(MA // PATCH, PATCH, MR // PATCH, PATCH).transpose(0, 2, 1, 3)
    spectrum = jnp.fft.fft2(patches, axes=(2, 3))
    magnitude = jnp.abs(spectrum)
    smooth = jnp.zeros_like(magnitude)
    for shift_a in (-1, 0, 1):
        for shift_b in (-1, 0, 1):
            smooth = smooth + jnp.roll(magnitude, (shift_a, shift_b), axis=(2, 3))
    weight = jnp.sqrt(smooth / 9.0)
    unscaled = jnp.fft.ifft2(spectrum * weight, axes=(2, 3)) * (PATCH * PATCH)
    power = lax.optimization_barrier(jnp.mean(jnp.abs(unscaled) ** 2, axis=(2, 3), keepdims=True))
    result = unscaled / jnp.sqrt(power + RMS_EPS)
    result = result.transpose(0, 2, 1, 3).reshape(MA, MR)
    return jnp.stack([jnp.real(result), jnp.imag(result)], axis=0)

def reference(epoch_image_tensor, along_track_shifts, cross_track_shifts, epoch_present_table):
    nwa = AZ // WIN
    nwr = RG // WIN
    primary_epoch = epoch_image_tensor[0].astype(jnp.float32)
    ref_amp = jnp.sqrt(primary_epoch[0] ** 2 + primary_epoch[1] ** 2)
    ref_win = ref_amp.reshape(nwa, WIN, nwr, WIN)
    ref_dev = ref_win - lax.optimization_barrier(jnp.mean(ref_win, axis=(1, 3), keepdims=True))
    ref_var = lax.optimization_barrier(jnp.mean(ref_dev ** 2, axis=(1, 3)))

    def lone_epoch(inputs):
        secondary, shift_rows, shift_cols, keep_flag = inputs
        padded = jnp.pad(secondary, ((0, 0), (MARGIN_LINES, MARGIN_LINES), (RHALO, RHALO)))
        row_start = (jnp.arange(nwa, dtype=jnp.int32) * WIN)[:, None] + MARGIN_LINES + shift_rows
        col_start = (jnp.arange(nwr, dtype=jnp.int32) * WIN)[None, :] + RHALO + shift_cols
        row_start = jnp.broadcast_to(row_start, (nwa, nwr)).astype(jnp.int32)
        col_start = jnp.broadcast_to(col_start, (nwa, nwr)).astype(jnp.int32)

        def cutout(start_a, start_r):
            return lax.dynamic_slice(padded, (jnp.int32(0), start_a, start_r), (2, WIN, WIN))
        tiles = jax.vmap(jax.vmap(cutout))(row_start, col_start)
        tiles = tiles * keep_flag.astype(tiles.dtype)[:, None, None, None, None]
        moved = tiles.astype(jnp.float32).transpose(2, 0, 3, 1, 4)
        sec_amp = jnp.sqrt(moved[0] ** 2 + moved[1] ** 2)
        sec_dev = sec_amp - lax.optimization_barrier(jnp.mean(sec_amp, axis=(1, 3), keepdims=True))
        sec_var = lax.optimization_barrier(jnp.mean(sec_dev ** 2, axis=(1, 3)))
        covariance = lax.optimization_barrier(jnp.mean(ref_dev * sec_dev, axis=(1, 3)))
        corr = covariance / jnp.sqrt((ref_var + VAR_EPS) * (sec_var + VAR_EPS))
        moved = moved.reshape(2, AZ, RG)
        ifg_real = primary_epoch[0] * moved[0] + primary_epoch[1] * moved[1]
        ifg_imag = primary_epoch[1] * moved[0] - primary_epoch[0] * moved[1]
        ifg = jnp.stack([ifg_real, ifg_imag], axis=0)
        looks = ifg.reshape(2, AZ // LOOK_AZ, LOOK_AZ, RG // LOOK_RG, LOOK_RG).sum(axis=(2, 4))
        return (corr, goldstein(looks))
    tile_similarity, smoothed_ifgs = lax.map(lone_epoch, (epoch_image_tensor, along_track_shifts, cross_track_shifts, epoch_present_table))
    return (tile_similarity, smoothed_ifgs)
```

```python
import jax
import jax.numpy as jnp
import numpy as np
from jax import lax
from jax.experimental import pallas as pl
from jax.experimental.pallas import tpu as pltpu
from jax.sharding import PartitionSpec as P

WIN = 64
MARGIN = 32
LOOK_AZ = 5
LOOK_RG = 20
PATCH = 32
LANES = 128
PIECE = 16
LAG = 3
PACE = 3

VAR_EPS = 1e-05
RMS_EPS = 1e-06
TINY = 1e-37

F32 = jnp.float32
BF16 = jnp.bfloat16


def tables(samples):
    turns = np.outer(np.arange(PATCH), np.arange(PATCH)) % PATCH
    angles = turns * (2.0 * np.pi / PATCH)
    two = np.eye(2)
    cosine = np.kron(two, np.cos(angles))
    sine = np.kron(two, np.sin(angles))
    rows_fwd = np.block([[cosine, sine], [-sine, cosine]])
    cols_fwd = np.block([[cosine, -sine], [sine, cosine]])
    dft = np.stack([rows_fwd, cols_fwd]).astype(np.float32)
    near = np.abs(np.arange(PATCH)[:, None] - np.arange(PATCH)[None, :])
    circular = np.minimum(near, PATCH - near) <= 1
    four = np.eye(LANES // PATCH)
    half = np.kron(np.eye(2), np.ones((WIN, WIN)))
    blocks = np.stack(
        [half, np.kron(four, circular), np.kron(four, np.ones((PATCH, PATCH)))]
    ).astype(np.float32)
    rg_pool = (
        np.arange(samples)[:, None] // LOOK_RG == np.arange(samples // LOOK_RG)[None, :]
    ).astype(np.float32)
    return (
        jnp.asarray(dft),
        jnp.asarray(blocks, BF16),
        jnp.asarray(rg_pool, BF16),
    )


def dot(a, b):
    return jnp.dot(a, b, preferred_element_type=F32)


def dot_high(a, b):
    a_high, a_low = split(a)
    b_high, b_low = split(b)
    return dot(a_high, b_high) + (dot(a_high, b_low) + dot(a_low, b_high))


def split(x):
    high = x.astype(BF16)
    return high, (x - high.astype(F32)).astype(BF16)


def dot_right(x, ones):
    high, low = split(x)
    return dot(high, ones) + dot(low, ones)


def root(x):
    return x * lax.rsqrt(jnp.maximum(x, TINY))


def resample(p, d, sizes, at_ref, ct_ref, pr_ref, wide, shifted, devs, stats):
    dates, lines, strips = sizes
    lane = lax.broadcasted_iota(jnp.int32, (WIN, LANES), 1)
    first = lane < WIN
    near_low = lane < LANES - MARGIN
    near_high = lane < MARGIN
    present = pr_ref[d, p]
    here = pl.ds(pl.multiple_of(p * WIN, WIN), WIN)
    for m in range(strips):
        rows = []
        turns = []
        for q in (2 * m, 2 * m + 1):
            start = jnp.where(
                present != 0, p * WIN + MARGIN + at_ref[p, d, q], lines + 2 * MARGIN
            )
            rows.append(pl.ds(start, WIN))
            turns.append((LANES - ct_ref[p, d, q]) & (LANES - 1))
        part = []
        for c in range(2):
            even = wide[d, c, m, rows[0], :]
            below = wide[d, c, m - 1, rows[0], :] if m > 0 else jnp.zeros_like(even)
            odd = wide[d, c, m, rows[1], :]
            above = wide[d, c, m + 1, rows[1], :] if m + 1 < strips else jnp.zeros_like(odd)
            even = pltpu.roll(jnp.where(near_low, even, below).astype(BF16), turns[0], 1)
            odd = pltpu.roll(jnp.where(near_high, above, odd).astype(BF16), turns[1], 1)
            part.append(jnp.where(first, even, odd).astype(F32))
            shifted[d, c, m, here, :] = part[c]
        amp = root(part[0] * part[0] + part[1] * part[1]).reshape(WIN // 8, 8, LANES)
        mean = jnp.sum(amp, axis=0) * (8.0 / WIN)
        dev = amp - mean[None]
        devs[d, m, here, :] = dev.reshape(WIN, LANES)
        stats[p, 0, m, d] = mean
        stats[p, 1, m, d] = jnp.sum(dev * dev, axis=0)


def prepare(p, sizes, ref, ref32, devs, stats):
    dates, lines, strips = sizes
    here = pl.ds(pl.multiple_of(p * WIN, WIN), WIN)
    for m in range(strips):
        cols = slice(m * LANES, (m + 1) * LANES)
        real = ref[0, here, cols].astype(F32)
        imag = ref[1, here, cols].astype(F32)
        ref32[0, m, here, :] = real
        ref32[1, m, here, :] = imag
        amp = root(real * real + imag * imag).reshape(WIN // 8, 8, LANES)
        mean = jnp.sum(amp, axis=0) * (8.0 / WIN)
        dev = amp - mean[None]
        stats[p, 0, m, dates] = mean
        stats[p, 1, m, dates] = jnp.sum(dev * dev, axis=0)
        for d in range(dates):
            joint = devs[d, m, here, :].reshape(WIN // 8, 8, LANES) * dev
            stats[p, 2, m, d] = jnp.sum(joint, axis=0)


def similarity(p, sizes, blk_ref, stats, sim_ref):
    dates, lines, strips = sizes
    half = blk_ref[0]

    def total(x):
        flat = x.reshape(-1, LANES)
        return jnp.sum(dot_right(flat, half).reshape(-1, 8, LANES), axis=1, keepdims=True)

    count = 8.0 * WIN
    means = stats[p, 0].reshape(strips * (dates + 1), 8, LANES)
    away = means - total(means) * (1.0 / count)
    spread = stats[p, 1].reshape(strips * (dates + 1), 8, LANES)
    var = total(spread + (WIN / 8.0) * (away * away)) * (1.0 / (WIN * WIN))
    away = away.reshape(strips, dates + 1, 8, LANES)
    var = var.reshape(strips, dates + 1, 1, LANES)
    joint = stats[p, 2][:, :dates] + (WIN / 8.0) * (away[:, :dates] * away[:, dates:])
    cov = total(joint).reshape(strips, dates, 1, LANES) * (1.0 / (WIN * WIN))
    corr = cov / jnp.sqrt((var[:, dates:] + VAR_EPS) * (var[:, :dates] + VAR_EPS))
    lane = lax.broadcasted_iota(jnp.int32, (dates, 1, LANES), 2)
    found = jnp.zeros((dates, 1, LANES), F32)
    for m in range(strips):
        here = corr[m]
        other = pltpu.roll(here.reshape(dates, LANES), WIN, 1).reshape(dates, 1, LANES)
        left = jnp.where(lane < WIN, here, other)
        right = jnp.where(lane < WIN, other, here)
        found = jnp.where(lane == 2 * m, left, jnp.where(lane == 2 * m + 1, right, found))
    sim_ref[p] = found.reshape(dates, LANES)[:, : sim_ref.shape[2]]


def interferogram(g, sizes, rgp_ref, ref32, shifted, prod, pooled):
    dates, lines, strips = sizes
    rows = [pl.ds(g * (8 * LOOK_AZ) + k, 8, stride=LOOK_AZ) for k in range(LOOK_AZ)]
    for m in range(strips):
        cols = slice(m * LANES, (m + 1) * LANES)
        rr = [ref32[0, m, at, :] for at in rows]
        ri = [ref32[1, m, at, :] for at in rows]
        for d in range(dates):
            real = imag = 0.0
            for k, at in enumerate(rows):
                sr = shifted[d, 0, m, at, :]
                si = shifted[d, 1, m, at, :]
                real = real + (rr[k] * sr + ri[k] * si)
                imag = imag + (ri[k] * sr - rr[k] * si)
            high, low = split(jnp.concatenate([real, imag], axis=0))
            prod[0, d, :, cols] = high
            prod[1, d, :, cols] = low
    sums = dot(prod[...].reshape(2 * dates * 16, strips * LANES), rgp_ref[...])
    sums = (sums[: dates * 16] + sums[dates * 16 :]).reshape(dates, 2, 8, -1)
    groups = PATCH // 8
    at = pl.ds(pl.multiple_of((g % groups) * 8, 8), 8)
    for d in range(dates):
        for c in range(2):
            pooled[g // groups, d // 2, c, d % 2, at, :] = sums[d, c]


def goldstein(h, dates, out_ref, dft_ref, blk_ref, pooled):
    rows_fwd = dft_ref[0]
    cols_fwd = dft_ref[1]
    pairs = dates // 2

    def rows_to_cols(x):
        return jnp.concatenate([x[:WIN], x[WIN:]], axis=1)

    turned = []
    for e in range(pairs):
        z = pooled[h, e].reshape(2 * WIN, -1)
        turned.append(rows_to_cols(dot_high(rows_fwd, z)))
    spectrum = dot_high(jnp.concatenate(turned, axis=0), cols_fwd)
    squares = spectrum * spectrum
    magnitude = root(squares + pltpu.roll(squares, WIN, 1))
    smooth = dot_right(magnitude, blk_ref[1]).reshape(-1, PATCH, LANES)
    smooth = (
        smooth
        + jnp.concatenate([smooth[:, 1:], smooth[:, :1]], axis=1)
        + jnp.concatenate([smooth[:, -1:], smooth[:, :-1]], axis=1)
    ).reshape(spectrum.shape)
    weighted = spectrum * root(smooth * (1.0 / 9.0))
    turned = []
    for e in range(pairs):
        w = weighted[e * WIN : (e + 1) * WIN]
        w = jnp.concatenate([w[:, :WIN], w[:, WIN:]], axis=0)
        turned.append(rows_to_cols(dot_high(cols_fwd, w)))
    back = dot_high(jnp.concatenate(turned, axis=0), rows_fwd)
    squares = back * back
    power = dot_right(squares + pltpu.roll(squares, WIN, 1), blk_ref[2]).reshape(-1, PATCH, LANES)
    power = jnp.sum(power, axis=1, keepdims=True) * (1.0 / (PATCH * PATCH))
    scaled = back.reshape(-1, PATCH, LANES) * lax.rsqrt(power + RMS_EPS)
    at = pl.ds(pl.multiple_of(h * PATCH, PATCH), PATCH)
    for d in range(dates):
        out_ref[d, 0, at, :] = scaled[d][:, :WIN]
        out_ref[d, 1, at, :] = scaled[d][:, WIN:]


def ring_device(position, count):
    half = count // 2
    return jnp.where(position < half, 2 * position, 2 * (count - 1 - position) + 1)


def kernel(
    at_ref, ct_ref, pr_ref, img_ref, dft_ref, blk_ref, rgp_ref,
    sim_ref, out_ref,
    image, halo, ref, wide, shifted, devs, ref32, prod, pooled, stats,
    image_sem, root_sem, halo_send, halo_recv, ref_send, ref_recv,
):
    dates, _, lines, samples = img_ref.shape
    strips = samples // LANES
    rows = lines // WIN
    pieces = ref_send.shape[1]
    height = lines // pieces
    each = WIN // height
    groups = lines // (8 * LOOK_AZ)
    halves = lines // (LOOK_AZ * PATCH)
    sizes = (dates, lines, strips)
    count = lax.axis_size("date")
    az_count = lax.axis_size("az")
    az = lax.axis_index("az")
    mine = lax.axis_index("date")
    position = jnp.where(mine % 2 == 0, mine // 2, count - 1 - mine // 2)
    after = ring_device((position + 1) % count, count)
    before = ring_device((position + count - 1) % count, count)
    hops = (position, (count - position) % count)
    targets = (after, before)
    mesh_ids = pl.DeviceIdType.MESH

    def load(i):
        d = i // 2
        c = i % 2
        return pltpu.make_async_copy(img_ref.at[d, c], image.at[d, c], image_sem.at[i])

    for i in range(2 * dates):
        load(i).start()
    own = pltpu.make_async_copy(img_ref.at[0], ref, root_sem)

    @pl.when(mine == 0)
    def _():
        own.start()

    barrier = pltpu.get_barrier_semaphore()
    for target in targets:
        pl.semaphore_signal(barrier, inc=1, device_id={"date": target}, device_id_type=mesh_ids)

    @pl.when(az > 0)
    def _():
        pl.semaphore_signal(barrier, inc=1, device_id={"az": az - 1}, device_id_type=mesh_ids)

    @pl.when(az < az_count - 1)
    def _():
        pl.semaphore_signal(barrier, inc=1, device_id={"az": az + 1}, device_id_type=mesh_ids)

    peers = 2 + jnp.where(az > 0, 1, 0) + jnp.where(az < az_count - 1, 1, 0)
    pl.semaphore_wait(barrier, peers)

    def relay(c, j, first):
        at = pl.ds(pl.multiple_of(j * height, height), height)
        return pltpu.make_async_remote_copy(
            src_ref=img_ref.at[0, c, at] if first else ref.at[c, at],
            dst_ref=ref.at[c, at],
            send_sem=ref_send.at[c, j],
            recv_sem=ref_recv.at[c, j],
            device_id={"date": targets[c]},
            device_id_type=mesh_ids,
        )

    @pl.when(mine == 0)
    def _():
        def launch(j, carry):
            for c in range(2):
                relay(c, j, True).start()
            return carry

        lax.fori_loop(0, pieces, launch, 0)

    def slot(t):
        for c in range(2):
            j = t - (hops[c] - 1) * LAG

            @pl.when((hops[c] > 0) & (hops[c] < count - 1) & (j >= 0) & (j < pieces))
            def _():
                relay(c, j, False).wait_recv()
                relay(c, j, False).start()

    def edge(k):
        start = 0 if k else lines - MARGIN
        return pltpu.make_async_remote_copy(
            src_ref=img_ref.at[:, :, pl.ds(start, MARGIN)],
            dst_ref=halo.at[k],
            send_sem=halo_send.at[k],
            recv_sem=halo_recv.at[k],
            device_id={"az": az - 1 if k else az + 1},
            device_id_type=mesh_ids,
        )

    sends = (az < az_count - 1, az > 0)
    takes = (az > 0, az < az_count - 1)
    for k in range(2):
        @pl.when(sends[k])
        def _():
            edge(k).start()

    def widen(i, carry):
        d = i // 2
        c = i % 2
        load(i).wait()
        for m in range(strips):
            cols = slice(m * LANES, (m + 1) * LANES)
            wide[d, c, m, MARGIN : MARGIN + lines, :] = image[d, c, :, cols].astype(F32)
            wide[d, c, m, 2 * MARGIN + lines : 2 * MARGIN + lines + WIN, :] = jnp.zeros((WIN, LANES), F32)
        return carry

    lax.fori_loop(0, 2 * dates, widen, 0)
    slot(0)

    def fringe(k):
        first = MARGIN + lines if k else 0

        @pl.when(takes[k])
        def _():
            edge(k).wait_recv()

            def convert(i, carry):
                d = i // 2
                c = i % 2
                for m in range(strips):
                    cols = slice(m * LANES, (m + 1) * LANES)
                    wide[d, c, m, first : first + MARGIN, :] = halo[k, d, c, :, cols].astype(F32)
                return carry

            lax.fori_loop(0, 2 * dates, convert, 0)

        @pl.when(jnp.logical_not(takes[k]))
        def _():
            def clear(i, carry):
                for m in range(strips):
                    wide[i // 2, i % 2, m, first : first + MARGIN, :] = jnp.zeros((MARGIN, LANES), F32)
                return carry

            lax.fori_loop(0, 2 * dates, clear, 0)

    def shift(i, carry):
        s = i // dates

        @pl.when((i % PACE) == 0)
        def _():
            slot(1 + i // PACE)

        @pl.when(i == (rows - 2) * dates)
        def _():
            for k in range(2):
                fringe(k)

        p = jnp.where(s < rows - 2, s + 1, jnp.where(s == rows - 2, 0, rows - 1))
        resample(p, i % dates, sizes, at_ref, ct_ref, pr_ref, wide, shifted, devs, stats)
        return carry

    lax.fori_loop(0, dates * rows, shift, 0)

    @pl.when(mine == 0)
    def _():
        own.wait()

    begun = 1 + -(-dates * rows // PACE)
    last = pieces + max(0, count - 3) * LAG

    def window_of(g):
        return (g * (8 * LOOK_AZ) + 8 * LOOK_AZ - 1) // WIN

    def due(g):
        ready = jnp.minimum(last, (window_of(g) + 1) * each + (count - 2) * LAG)
        return jnp.where(g < 0, begun, jnp.maximum(begun, ready))

    def group(g):
        p = window_of(g)

        def forward(t, carry):
            slot(t)
            return carry

        lax.fori_loop(due(g - 1), due(g), forward, 0)

        @pl.when((g == 0) | (p > window_of(g - 1)))
        def _():
            for c in range(2):
                @pl.when(hops[c] == count - 1)
                def _():
                    for e in range(each):
                        relay(c, p * each + e, False).wait_recv()

            prepare(p, sizes, ref, ref32, devs, stats)
            similarity(p, sizes, blk_ref, stats, sim_ref)

        interferogram(g, sizes, rgp_ref, ref32, shifted, prod, pooled)

    def patches(h, carry):
        share = groups // halves

        def one(i, inner):
            group(h * share + i)
            return inner

        lax.fori_loop(0, share, one, 0)
        goldstein(h, dates, out_ref, dft_ref, blk_ref, pooled)
        return carry

    lax.fori_loop(0, halves, patches, 0)

    for c in range(2):
        @pl.when(hops[c] < count - 1)
        def _():
            def drain(j, carry):
                relay(c, j, False).wait_send()
                return carry

            lax.fori_loop(0, pieces, drain, 0)

    for k in range(2):
        @pl.when(sends[k])
        def _():
            edge(k).wait_send()


def on_device(image, along, cross, present):
    dates, _, lines, samples = image.shape
    strips = samples // LANES
    rows = lines // WIN
    pieces = lines // PIECE
    halves = lines // (LOOK_AZ * PATCH)
    smem = pl.BlockSpec(memory_space=pltpu.SMEM)
    vmem = pl.BlockSpec(memory_space=pltpu.VMEM)
    dma = pltpu.SemaphoreType.DMA
    dft, blocks, rg_pool = tables(samples)
    found, filtered = pl.pallas_call(
        kernel,
        out_shape=(
            jax.ShapeDtypeStruct((rows, dates, samples // WIN), F32),
            jax.ShapeDtypeStruct((dates, 2, lines // LOOK_AZ, samples // LOOK_RG), F32),
        ),
        in_specs=[smem] * 3 + [pl.BlockSpec(memory_space=pl.ANY)] + [vmem] * 3,
        out_specs=(vmem, vmem),
        scratch_shapes=[
            pltpu.VMEM((dates, 2, lines, samples), BF16),
            pltpu.VMEM((2, dates, 2, MARGIN, samples), BF16),
            pltpu.VMEM((2, lines, samples), BF16),
            pltpu.VMEM((dates, 2, strips, lines + 2 * MARGIN + WIN, LANES), F32),
            pltpu.VMEM((dates, 2, strips, lines, LANES), F32),
            pltpu.VMEM((dates, strips, lines, LANES), F32),
            pltpu.VMEM((2, strips, lines, LANES), F32),
            pltpu.VMEM((2, dates, 16, samples), BF16),
            pltpu.VMEM((halves, dates // 2, 2, 2, PATCH, samples // LOOK_RG), F32),
            pltpu.VMEM((rows, 3, strips, dates + 1, 8, LANES), F32),
            dma((2 * dates,)),
            dma(()),
            dma((2,)),
            dma((2,)),
            dma((2, pieces)),
            dma((2, pieces)),
        ],
        compiler_params=pltpu.CompilerParams(
            vmem_limit_bytes=62 * 1024 * 1024, collective_id=0, has_side_effects=True
        ),
    )(
        along.transpose(1, 0, 2), cross.transpose(1, 0, 2), present, image, dft, blocks, rg_pool
    )
    return found.transpose(1, 0, 2), filtered


def solution(mesh):
    placed = (
        P("date", None, "az", None),
        P("date", "az", None),
        P("date", "az", None),
        P("date", "az"),
    )
    return jax.shard_map(
        on_device,
        mesh=mesh,
        in_specs=placed,
        out_specs=(P("date", "az", None), P("date", None, "az", None)),
        check_vma=False,
    )
```

```python
import jax
import jax.numpy as jnp
import numpy as np
from jax import lax
from jax.experimental import pallas as pl
from jax.experimental.pallas import tpu as pltpu
from jax.sharding import PartitionSpec as P

WIN = 64
MARGIN = 32
LOOK_AZ = 5
LOOK_RG = 20
PATCH = 32
LANES = 128
PIECE = 16
LAG = 3
PACE = 3
HALO_SLOT = 9
DUP = 3

VAR_EPS = 1e-05
RMS_EPS = 1e-06
TINY = 1e-37

F32 = jnp.float32
BF16 = jnp.bfloat16


def tables(samples):
    turns = np.outer(np.arange(PATCH), np.arange(PATCH)) % PATCH
    angles = turns * (2.0 * np.pi / PATCH)
    two = np.eye(2)
    cosine = np.kron(two, np.cos(angles))
    sine = np.kron(two, np.sin(angles))
    rows_fwd = np.block([[cosine, sine], [-sine, cosine]])
    cols_fwd = np.block([[cosine, -sine], [sine, cosine]])
    dft = np.stack([rows_fwd, cols_fwd]).astype(np.float32)
    near = np.abs(np.arange(PATCH)[:, None] - np.arange(PATCH)[None, :])
    circular = np.minimum(near, PATCH - near) <= 1
    four = np.eye(LANES // PATCH)
    half = np.kron(np.eye(2), np.ones((WIN, WIN)))
    blocks = np.stack(
        [half, np.kron(four, circular), np.kron(four, np.ones((PATCH, PATCH)))]
    ).astype(np.float32)
    rg_pool = (
        np.arange(samples)[:, None] // LOOK_RG == np.arange(samples // LOOK_RG)[None, :]
    ).astype(np.float32)
    return (
        jnp.asarray(dft),
        jnp.asarray(blocks, BF16),
        jnp.asarray(rg_pool, BF16),
    )


def dot(a, b):
    return jnp.dot(a, b, preferred_element_type=F32)


def dot_high(a, b):
    a_high, a_low = split(a)
    b_high, b_low = split(b)
    return dot(a_high, b_high) + (dot(a_high, b_low) + dot(a_low, b_high))


def split(x):
    high = x.astype(BF16)
    return high, (x - high.astype(F32)).astype(BF16)


def dot_right(x, ones):
    high, low = split(x)
    return dot(high, ones) + dot(low, ones)


def root(x):
    return x * lax.rsqrt(jnp.maximum(x, TINY))


def resample(p, d, sizes, at_ref, ct_ref, pr_ref, wide, shifted, devs, stats):
    dates, lines, strips = sizes
    lane = lax.broadcasted_iota(jnp.int32, (WIN, LANES), 1)
    first = lane < WIN
    near_low = lane < LANES - MARGIN
    near_high = lane < MARGIN
    present = pr_ref[d, p]
    here = pl.ds(pl.multiple_of(p * WIN, WIN), WIN)
    for m in range(strips):
        rows = []
        turns = []
        for q in (2 * m, 2 * m + 1):
            start = jnp.where(
                present != 0, p * WIN + MARGIN + at_ref[p, d, q], lines + 2 * MARGIN
            )
            rows.append(pl.ds(start, WIN))
            turns.append((LANES - ct_ref[p, d, q]) & (LANES - 1))
        part = []
        for c in range(2):
            even = wide[d, c, m, rows[0], :]
            below = wide[d, c, m - 1, rows[0], :] if m > 0 else jnp.zeros_like(even)
            odd = wide[d, c, m, rows[1], :]
            above = wide[d, c, m + 1, rows[1], :] if m + 1 < strips else jnp.zeros_like(odd)
            even = pltpu.roll(jnp.where(near_low, even, below).astype(BF16), turns[0], 1)
            odd = pltpu.roll(jnp.where(near_high, above, odd).astype(BF16), turns[1], 1)
            part.append(jnp.where(first, even, odd).astype(F32))
            shifted[d, c, m, here, :] = part[c]
        amp = root(part[0] * part[0] + part[1] * part[1]).reshape(WIN // 8, 8, LANES)
        mean = jnp.sum(amp, axis=0) * (8.0 / WIN)
        dev = amp - mean[None]
        devs[d, m, here, :] = dev.reshape(WIN, LANES)
        stats[p, 0, m, d] = mean
        stats[p, 1, m, d] = jnp.sum(dev * dev, axis=0)


def prepare(p, sizes, ref, ref32, devs, stats):
    dates, lines, strips = sizes
    here = pl.ds(pl.multiple_of(p * WIN, WIN), WIN)
    for m in range(strips):
        cols = slice(m * LANES, (m + 1) * LANES)
        real = ref[0, here, cols].astype(F32)
        imag = ref[1, here, cols].astype(F32)
        ref32[0, m, here, :] = real
        ref32[1, m, here, :] = imag
        amp = root(real * real + imag * imag).reshape(WIN // 8, 8, LANES)
        mean = jnp.sum(amp, axis=0) * (8.0 / WIN)
        dev = amp - mean[None]
        stats[p, 0, m, dates] = mean
        stats[p, 1, m, dates] = jnp.sum(dev * dev, axis=0)
        for d in range(dates):
            joint = devs[d, m, here, :].reshape(WIN // 8, 8, LANES) * dev
            stats[p, 2, m, d] = jnp.sum(joint, axis=0)


def similarity(p, sizes, blk_ref, stats, sim_ref):
    dates, lines, strips = sizes
    half = blk_ref[0]

    def total(x):
        flat = x.reshape(-1, LANES)
        return jnp.sum(dot_right(flat, half).reshape(-1, 8, LANES), axis=1, keepdims=True)

    count = 8.0 * WIN
    means = stats[p, 0].reshape(strips * (dates + 1), 8, LANES)
    away = means - total(means) * (1.0 / count)
    spread = stats[p, 1].reshape(strips * (dates + 1), 8, LANES)
    var = total(spread + (WIN / 8.0) * (away * away)) * (1.0 / (WIN * WIN))
    away = away.reshape(strips, dates + 1, 8, LANES)
    var = var.reshape(strips, dates + 1, 1, LANES)
    joint = stats[p, 2][:, :dates] + (WIN / 8.0) * (away[:, :dates] * away[:, dates:])
    cov = total(joint).reshape(strips, dates, 1, LANES) * (1.0 / (WIN * WIN))
    corr = cov / jnp.sqrt((var[:, dates:] + VAR_EPS) * (var[:, :dates] + VAR_EPS))
    lane = lax.broadcasted_iota(jnp.int32, (dates, 1, LANES), 2)
    found = jnp.zeros((dates, 1, LANES), F32)
    for m in range(strips):
        here = corr[m]
        other = pltpu.roll(here.reshape(dates, LANES), WIN, 1).reshape(dates, 1, LANES)
        left = jnp.where(lane < WIN, here, other)
        right = jnp.where(lane < WIN, other, here)
        found = jnp.where(lane == 2 * m, left, jnp.where(lane == 2 * m + 1, right, found))
    sim_ref[p] = found.reshape(dates, LANES)[:, : sim_ref.shape[2]]


def interferogram(g, sizes, rgp_ref, ref32, shifted, prod, pooled):
    dates, lines, strips = sizes
    rows = [pl.ds(g * (8 * LOOK_AZ) + k, 8, stride=LOOK_AZ) for k in range(LOOK_AZ)]
    for m in range(strips):
        cols = slice(m * LANES, (m + 1) * LANES)
        rr = [ref32[0, m, at, :] for at in rows]
        ri = [ref32[1, m, at, :] for at in rows]
        for d in range(dates):
            real = imag = 0.0
            for k, at in enumerate(rows):
                sr = shifted[d, 0, m, at, :]
                si = shifted[d, 1, m, at, :]
                real = real + (rr[k] * sr + ri[k] * si)
                imag = imag + (ri[k] * sr - rr[k] * si)
            high, low = split(jnp.concatenate([real, imag], axis=0))
            prod[0, d, :, cols] = high
            prod[1, d, :, cols] = low
    sums = dot(prod[...].reshape(2 * dates * 16, strips * LANES), rgp_ref[...])
    sums = (sums[: dates * 16] + sums[dates * 16 :]).reshape(dates, 2, 8, -1)
    groups = PATCH // 8
    at = pl.ds(pl.multiple_of((g % groups) * 8, 8), 8)
    for d in range(dates):
        for c in range(2):
            pooled[d // 2, c, d % 2, at, :] = sums[d, c]


def goldstein(h, dates, out_ref, dft_ref, blk_ref, pooled):
    rows_fwd = dft_ref[0]
    cols_fwd = dft_ref[1]
    pairs = dates // 2

    def rows_to_cols(x):
        return jnp.concatenate([x[:WIN], x[WIN:]], axis=1)

    turned = []
    for e in range(pairs):
        z = pooled[e].reshape(2 * WIN, -1)
        turned.append(rows_to_cols(dot_high(rows_fwd, z)))
    spectrum = dot_high(jnp.concatenate(turned, axis=0), cols_fwd)
    squares = spectrum * spectrum
    magnitude = root(squares + pltpu.roll(squares, WIN, 1))
    smooth = dot_right(magnitude, blk_ref[1]).reshape(-1, PATCH, LANES)
    smooth = (
        smooth
        + jnp.concatenate([smooth[:, 1:], smooth[:, :1]], axis=1)
        + jnp.concatenate([smooth[:, -1:], smooth[:, :-1]], axis=1)
    ).reshape(spectrum.shape)
    weighted = spectrum * root(smooth * (1.0 / 9.0))
    squares = weighted * weighted
    power = jnp.sum((squares + pltpu.roll(squares, WIN, 1)).reshape(-1, PATCH // 8, 8, LANES), axis=1)
    power = dot_right(power.reshape(-1, LANES), blk_ref[2]).reshape(-1, 8, LANES)
    scale = lax.rsqrt(jnp.sum(power, axis=1, keepdims=True) + RMS_EPS)
    turned = []
    for e in range(pairs):
        w = weighted[e * WIN : (e + 1) * WIN]
        w = jnp.concatenate([w[:, :WIN], w[:, WIN:]], axis=0)
        turned.append(rows_to_cols(dot_high(cols_fwd, w)))
    back = dot_high(jnp.concatenate(turned, axis=0), rows_fwd)
    scaled = back.reshape(-1, PATCH, LANES) * scale
    at = pl.ds(pl.multiple_of(h * PATCH, PATCH), PATCH)
    for d in range(dates):
        out_ref[d, 0, at, :] = scaled[d][:, :WIN]
        out_ref[d, 1, at, :] = scaled[d][:, WIN:]


def ring_device(position, count):
    half = count // 2
    return jnp.where(position < half, 2 * position, 2 * (count - 1 - position) + 1)


def kernel(
    at_hbm, ct_hbm, pr_hbm, img_ref, dft_hbm, blk_hbm, rgp_hbm,
    sim_ref, out_ref, pooled,
    image, halo, ref, wide, shifted, devs, ref32, prod, stats,
    at_ref, ct_ref, pr_ref, dft_ref, blk_ref, rgp_ref,
    image_sem, root_sem, table_sem, halo_send, halo_recv, ref_send, ref_recv, dup_send,
):
    dates, _, lines, samples = img_ref.shape
    strips = samples // LANES
    rows = lines // WIN
    pieces = ref_send.shape[1]
    height = lines // pieces
    each = WIN // height
    groups = lines // (8 * LOOK_AZ)
    halves = lines // (LOOK_AZ * PATCH)
    sizes = (dates, lines, strips)
    count = lax.axis_size("date")
    az_count = lax.axis_size("az")
    az = lax.axis_index("az")
    mine = lax.axis_index("date")
    position = jnp.where(mine % 2 == 0, mine // 2, count - 1 - mine // 2)
    after = ring_device((position + 1) % count, count)
    before = ring_device((position + count - 1) % count, count)
    hops = (position, (count - position) % count)
    targets = (after, before)
    mesh_ids = pl.DeviceIdType.MESH

    def load(i):
        d = i // 2
        c = i % 2
        return pltpu.make_async_copy(img_ref.at[d, c], image.at[d, c], image_sem.at[i])

    for i in range(2 * dates):
        load(i).start()
    pairs = (
        (at_hbm, at_ref), (ct_hbm, ct_ref), (pr_hbm, pr_ref),
        (dft_hbm, dft_ref), (blk_hbm, blk_ref), (rgp_hbm, rgp_ref),
    )
    extras = [pltpu.make_async_copy(a, b, table_sem.at[i]) for i, (a, b) in enumerate(pairs)]
    for copy in extras:
        copy.start()
    own = pltpu.make_async_copy(img_ref.at[0], ref, root_sem)

    @pl.when(mine == 0)
    def _():
        own.start()

    barrier = pltpu.get_barrier_semaphore()
    for target in targets:
        pl.semaphore_signal(barrier, inc=1, device_id={"date": target}, device_id_type=mesh_ids)

    @pl.when(az > 0)
    def _():
        pl.semaphore_signal(barrier, inc=1, device_id={"az": az - 1}, device_id_type=mesh_ids)

    @pl.when(az < az_count - 1)
    def _():
        pl.semaphore_signal(barrier, inc=1, device_id={"az": az + 1}, device_id_type=mesh_ids)

    peers = 2 + jnp.where(az > 0, 1, 0) + jnp.where(az < az_count - 1, 1, 0)
    pl.semaphore_wait(barrier, peers)

    def relay(c, j, first):
        at = pl.ds(pl.multiple_of(j * height, height), height)
        return pltpu.make_async_remote_copy(
            src_ref=img_ref.at[0, c, at] if first else ref.at[c, at],
            dst_ref=ref.at[c, at],
            send_sem=ref_send.at[c, j],
            recv_sem=ref_recv.at[c, j],
            device_id={"date": targets[c]},
            device_id_type=mesh_ids,
        )

    dups = DUP if count > 2 else 0

    def direct(c, e):
        at = pl.ds(lines - (dups - e) * height, height)
        return pltpu.make_async_remote_copy(
            src_ref=img_ref.at[0, c, at],
            dst_ref=ref.at[c, at],
            send_sem=dup_send.at[c, e],
            recv_sem=ref_recv.at[c, pieces - dups + e],
            device_id={"date": targets[1 - c]},
            device_id_type=mesh_ids,
        )

    @pl.when(mine == 0)
    def _():
        def launch(j, carry):
            for c in range(2):
                relay(c, j, True).start()
            return carry

        lax.fori_loop(0, pieces, launch, 0)
        for e in range(dups):
            for c in range(2):
                direct(c, e).start()

    def sent(c):
        return jnp.where(hops[c] == count - 2, pieces - dups, jnp.where(hops[c] == count - 1, 0, pieces))

    def slot(t):
        for c in range(2):
            j = t - (hops[c] - 1) * LAG

            here = (hops[c] > 0) & (hops[c] < count - 1) & (j >= 0) & (j < pieces)

            @pl.when(here)
            def _():
                relay(c, j, False).wait_recv()

            @pl.when(here & (j < sent(c)))
            def _():
                relay(c, j, False).start()

    def edge(k):
        start = 0 if k else lines - MARGIN
        return pltpu.make_async_remote_copy(
            src_ref=img_ref.at[:, :, pl.ds(start, MARGIN)],
            dst_ref=halo.at[k],
            send_sem=halo_send.at[k],
            recv_sem=halo_recv.at[k],
            device_id={"az": az - 1 if k else az + 1},
            device_id_type=mesh_ids,
        )

    sends = (az < az_count - 1, az > 0)
    takes = (az > 0, az < az_count - 1)
    for k in range(2):
        @pl.when(sends[k])
        def _():
            edge(k).start()

    def widen(i, carry):
        d = i // 2
        c = i % 2
        load(i).wait()
        for m in range(strips):
            cols = slice(m * LANES, (m + 1) * LANES)
            wide[d, c, m, MARGIN : MARGIN + lines, :] = image[d, c, :, cols].astype(F32)
            wide[d, c, m, 2 * MARGIN + lines : 2 * MARGIN + lines + WIN, :] = jnp.zeros((WIN, LANES), F32)
        return carry

    lax.fori_loop(0, 2 * dates, widen, 0)
    slot(0)

    def fringe(k):
        first = MARGIN + lines if k else 0

        @pl.when(takes[k])
        def _():
            edge(k).wait_recv()

            def convert(i, carry):
                d = i // 2
                c = i % 2
                for m in range(strips):
                    cols = slice(m * LANES, (m + 1) * LANES)
                    wide[d, c, m, first : first + MARGIN, :] = halo[k, d, c, :, cols].astype(F32)
                return carry

            lax.fori_loop(0, 2 * dates, convert, 0)

        @pl.when(jnp.logical_not(takes[k]))
        def _():
            def clear(i, carry):
                for m in range(strips):
                    wide[i // 2, i % 2, m, first : first + MARGIN, :] = jnp.zeros((MARGIN, LANES), F32)
                return carry

            lax.fori_loop(0, 2 * dates, clear, 0)

    for copy in extras[:3]:
        copy.wait()

    def forward(t, carry):
        slot(t)
        return carry

    def shift(first, begin):
        def one(i, carry):
            @pl.when((i % PACE) == 0)
            def _():
                slot(first + i // PACE)

            s = begin + i // dates
            p = jnp.where(s < rows - 2, s + 1, jnp.where(s == rows - 2, 0, rows - 1))
            resample(p, i % dates, sizes, at_ref, ct_ref, pr_ref, wide, shifted, devs, stats)
            return carry

        return one

    inner = dates * (rows - 2)
    lax.fori_loop(0, inner, shift(1, 0), 0)
    lax.fori_loop(1 + -(-inner // PACE), HALO_SLOT, forward, 0)
    for k in range(2):
        fringe(k)
    lax.fori_loop(0, 2 * dates, shift(HALO_SLOT, rows - 2), 0)

    @pl.when(mine == 0)
    def _():
        own.wait()

    for copy in extras[3:]:
        copy.wait()

    begun = HALO_SLOT + -(-2 * dates // PACE)
    last = pieces + max(0, count - 3) * LAG

    def window_of(g):
        return (g * (8 * LOOK_AZ) + 8 * LOOK_AZ - 1) // WIN

    def due(g, after):
        p = window_of(g)
        ready = jnp.maximum((p + 1) * each + (count - 2) * LAG, begun + 1 + g + p + after)
        return jnp.where(g < 0, begun, jnp.minimum(last, ready))

    def group(g):
        p = window_of(g)

        lax.fori_loop(due(g - 1, 1), due(g, 0), forward, 0)

        @pl.when((g == 0) | (p > window_of(g - 1)))
        def _():
            for c in range(2):
                @pl.when(hops[c] == count - 1)
                def _():
                    for e in range(each):
                        relay(c, p * each + e, False).wait_recv()

            prepare(p, sizes, ref, ref32, devs, stats)
            similarity(p, sizes, blk_ref, stats, sim_ref)

        lax.fori_loop(due(g, 0), due(g, 1), forward, 0)
        interferogram(g, sizes, rgp_ref, ref32, shifted, prod, pooled)

    def patches(h, carry):
        share = groups // halves

        def one(i, inner):
            group(h * share + i)
            return inner

        lax.fori_loop(0, share, one, 0)

        @pl.when(h < halves - 1)
        def _():
            goldstein(h, dates, out_ref, dft_ref, blk_ref, pooled)

        return carry

    lax.fori_loop(0, halves, patches, 0)

    for c in range(2):
        @pl.when(hops[c] < count - 1)
        def _():
            def drain(j, carry):
                relay(c, j, False).wait_send()
                return carry

            lax.fori_loop(0, sent(c), drain, 0)

    @pl.when(mine == 0)
    def _():
        for e in range(dups):
            for c in range(2):
                direct(c, e).wait_send()

    for k in range(2):
        @pl.when(sends[k])
        def _():
            edge(k).wait_send()


def finish(found_ref, early_ref, pooled_ref, dft_ref, blk_ref, sim_ref, out_ref):
    dates, _, early, _ = early_ref.shape
    sim_ref[...] = found_ref[...]
    out_ref[:, :, :early] = early_ref[...]
    goldstein(early // PATCH, dates, out_ref, dft_ref, blk_ref, pooled_ref)


def on_device(image, along, cross, present):
    dates, _, lines, samples = image.shape
    strips = samples // LANES
    rows = lines // WIN
    pieces = lines // PIECE
    halves = lines // (LOOK_AZ * PATCH)
    looks = samples // LOOK_RG
    vmem = pl.BlockSpec(memory_space=pltpu.VMEM)
    dma = pltpu.SemaphoreType.DMA
    dft, blocks, rg_pool = tables(samples)
    found, early, pooled = pl.pallas_call(
        kernel,
        out_shape=(
            jax.ShapeDtypeStruct((rows, dates, samples // WIN), F32),
            jax.ShapeDtypeStruct((dates, 2, (halves - 1) * PATCH, looks), F32),
            jax.ShapeDtypeStruct((dates // 2, 2, 2, PATCH, looks), F32),
        ),
        in_specs=[pl.BlockSpec(memory_space=pl.ANY)] * 7,
        out_specs=(vmem, vmem, vmem),
        scratch_shapes=[
            pltpu.VMEM((dates, 2, lines, samples), BF16),
            pltpu.VMEM((2, dates, 2, MARGIN, samples), BF16),
            pltpu.VMEM((2, lines, samples), BF16),
            pltpu.VMEM((dates, 2, strips, lines + 2 * MARGIN + WIN, LANES), F32),
            pltpu.VMEM((dates, 2, strips, lines, LANES), F32),
            pltpu.VMEM((dates, strips, lines, LANES), F32),
            pltpu.VMEM((2, strips, lines, LANES), F32),
            pltpu.VMEM((2, dates, 16, samples), BF16),
            pltpu.VMEM((rows, 3, strips, dates + 1, 8, LANES), F32),
            pltpu.SMEM((rows, dates, samples // WIN), jnp.int32),
            pltpu.SMEM((rows, dates, samples // WIN), jnp.int32),
            pltpu.SMEM((dates, rows), jnp.int32),
            pltpu.VMEM(dft.shape, F32),
            pltpu.VMEM(blocks.shape, BF16),
            pltpu.VMEM(rg_pool.shape, BF16),
            dma((2 * dates,)),
            dma(()),
            dma((6,)),
            dma((2,)),
            dma((2,)),
            dma((2, pieces)),
            dma((2, pieces)),
            dma((2, DUP)),
        ],
        compiler_params=pltpu.CompilerParams(
            vmem_limit_bytes=62 * 1024 * 1024, collective_id=0, has_side_effects=True
        ),
    )(
        along.transpose(1, 0, 2), cross.transpose(1, 0, 2), present, image, dft, blocks, rg_pool
    )
    found, filtered = pl.pallas_call(
        finish,
        out_shape=(
            jax.ShapeDtypeStruct(found.shape, F32),
            jax.ShapeDtypeStruct((dates, 2, lines // LOOK_AZ, looks), F32),
        ),
        in_specs=[vmem] * 5,
        out_specs=(vmem, vmem),
    )(found, early, pooled, dft, blocks)
    return found.transpose(1, 0, 2), filtered


def solution(mesh):
    placed = (
        P("date", None, "az", None),
        P("date", "az", None),
        P("date", "az", None),
        P("date", "az"),
    )
    return jax.shard_map(
        on_device,
        mesh=mesh,
        in_specs=placed,
        out_specs=(P("date", "az", None), P("date", None, "az", None)),
        check_vma=False,
    )
```

```python
import jax
import jax.numpy as jnp
import ml_dtypes
import numpy as np
from jax import lax
from jax.experimental import pallas as pl
from jax.experimental.pallas import tpu as pltpu
from jax.sharding import PartitionSpec as P

WIN = 64
MARGIN = 32
LOOK_AZ = 5
LOOK_RG = 20
PATCH = 32
LANES = 128
PIECE = 16
LAG = 4
PACE = 2
HALO_SLOT = 12
DUP = 3

VAR_EPS = 1e-05
RMS_EPS = 1e-06
TINY = 1e-37

F32 = jnp.float32
BF16 = jnp.bfloat16


def two_terms(x):
    x = x.astype(np.float32)
    high = x.astype(ml_dtypes.bfloat16)
    return high, (x - high.astype(np.float32)).astype(ml_dtypes.bfloat16)


def tables(dates, samples):
    turns = np.outer(np.arange(PATCH), np.arange(PATCH)) % PATCH
    angles = turns * (2.0 * np.pi / PATCH)
    two = np.eye(samples // LOOK_RG // PATCH)
    cosine = np.kron(two, np.cos(angles))
    sine = np.kron(two, np.sin(angles))
    each = np.eye(dates)
    left = np.concatenate([np.kron(each, np.cos(angles)), np.kron(each, np.sin(angles))], axis=1)
    right = np.block([[cosine, sine], [-sine, cosine]])
    near = np.abs(np.arange(PATCH)[:, None] - np.arange(PATCH)[None, :])
    circular = np.minimum(near, PATCH - near) <= 1
    four = np.eye(LANES // PATCH)
    half = np.kron(np.eye(2), np.ones((WIN, WIN)))
    blocks = np.stack([half, np.kron(four, circular), np.kron(four, np.ones((PATCH, PATCH)))])
    blocks = np.concatenate([blocks, blocks], axis=1)
    pool = np.arange(samples)[:, None] // LOOK_RG == np.arange(samples // LOOK_RG)[None, :]
    pool = pool.astype(np.float64) @ np.concatenate([cosine, -sine], axis=1)
    return (
        jnp.asarray(np.stack(two_terms(left))),
        jnp.asarray(np.concatenate(two_terms(right), axis=1)),
        jnp.asarray(blocks, BF16),
        jnp.asarray(np.concatenate(two_terms(pool), axis=1)),
    )


def dot(a, b):
    return jnp.dot(a, b, preferred_element_type=F32)


def split(x):
    high = x.astype(BF16)
    return high, (x - high.astype(F32)).astype(BF16)


def dot_right(x, ones):
    return dot(jnp.concatenate(split(x), axis=1), ones)


def turned(x, sign):
    return sign * pltpu.roll(x, WIN, 1)


def root(x):
    return x * lax.rsqrt(jnp.maximum(x, TINY))


def resample(p, d, sizes, at_ref, ct_ref, pr_ref, wide, shifted, devs, stats):
    dates, lines, strips = sizes
    lane = lax.broadcasted_iota(jnp.int32, (WIN, LANES), 1)
    first = lane < WIN
    near_low = lane < LANES - MARGIN
    near_high = lane < MARGIN
    present = pr_ref[d, p]
    here = pl.ds(pl.multiple_of(p * WIN, WIN), WIN)
    for m in range(strips):
        rows = []
        turns = []
        for q in (2 * m, 2 * m + 1):
            start = jnp.where(
                present != 0, p * WIN + MARGIN + at_ref[p, d, q], lines + 2 * MARGIN
            )
            rows.append(pl.ds(start, WIN))
            turns.append((LANES - ct_ref[p, d, q]) & (LANES - 1))
        part = []
        for c in range(2):
            even = wide[d, c, m, rows[0], :]
            below = wide[d, c, m - 1, rows[0], :] if m > 0 else jnp.zeros_like(even)
            odd = wide[d, c, m, rows[1], :]
            above = wide[d, c, m + 1, rows[1], :] if m + 1 < strips else jnp.zeros_like(odd)
            even = pltpu.roll(jnp.where(near_low, even, below).astype(BF16), turns[0], 1)
            odd = pltpu.roll(jnp.where(near_high, above, odd).astype(BF16), turns[1], 1)
            part.append(jnp.where(first, even, odd).astype(F32))
            shifted[d, c, m, here, :] = part[c]
        amp = root(part[0] * part[0] + part[1] * part[1]).reshape(WIN // 8, 8, LANES)
        mean = jnp.sum(amp, axis=0) * (8.0 / WIN)
        dev = amp - mean[None]
        devs[d, m, here, :] = dev.reshape(WIN, LANES)
        stats[p, 0, m, d] = mean
        stats[p, 1, m, d] = jnp.sum(dev * dev, axis=0)


def total(x, half):
    sums = dot_right(x.reshape(-1, LANES), half).reshape(-1, 8, LANES)
    return jnp.sum(sums, axis=1, keepdims=True)


def settle(p, sizes, blk_ref, stats):
    dates, lines, strips = sizes
    half = blk_ref[0]
    shape = (strips * dates, 8, LANES)
    means = stats[p, 0].reshape(shape)
    away = means - total(means, half) * (1.0 / (8.0 * WIN))
    spread = stats[p, 1].reshape(shape) + (WIN / 8.0) * (away * away)
    var = total(spread, half) * (1.0 / (WIN * WIN))
    stats[p, 0] = away.reshape(strips, dates, 8, LANES)
    stats[p, 1] = jnp.broadcast_to(var + VAR_EPS, shape).reshape(strips, dates, 8, LANES)


def prepare(p, e, height, sizes, ref, ref32, devs, stats, own):
    dates, lines, strips = sizes
    here = pl.ds(pl.multiple_of(p * WIN + e * height, height), height)
    fresh = e == 0
    for m in range(strips):
        cols = slice(m * LANES, (m + 1) * LANES)
        real = ref[0, here, cols].astype(F32)
        imag = ref[1, here, cols].astype(F32)
        ref32[0, m, here, :] = real
        ref32[1, m, here, :] = imag
        amp = root(real * real + imag * imag).reshape(height // 8, 8, LANES)
        pivot = jnp.where(fresh, amp[0], own[p, 0, m])
        own[p, 0, m] = pivot
        dev = amp - pivot[None]
        own[p, 1, m] = jnp.sum(dev, axis=0) + jnp.where(fresh, 0.0, own[p, 1, m])
        own[p, 2, m] = jnp.sum(dev * dev, axis=0) + jnp.where(fresh, 0.0, own[p, 2, m])
        for d in range(dates):
            joint = devs[d, m, here, :].reshape(height // 8, 8, LANES) * dev
            stats[p, 2, m, d] = jnp.sum(joint, axis=0) + jnp.where(fresh, 0.0, stats[p, 2, m, d])


def similarity(p, sizes, blk_ref, stats, own, sim_ref):
    dates, lines, strips = sizes
    half = blk_ref[0]
    first = own[p, 1]
    means = own[p, 0] + first * (8.0 / WIN)
    away = means - total(means, half) * (1.0 / (8.0 * WIN))
    spread = own[p, 2] - first * first * (8.0 / WIN) + (WIN / 8.0) * (away * away)
    joint = stats[p, 2] + (WIN / 8.0) * (stats[p, 0] * away[:, None])
    every = jnp.concatenate([spread, joint.reshape(strips * dates, 8, LANES)], axis=0)
    every = total(every, half) * (1.0 / (WIN * WIN))
    var = every[:strips].reshape(strips, 1, 1, LANES)
    cov = every[strips:].reshape(strips, dates, 1, LANES)
    corr = cov * lax.rsqrt((var + VAR_EPS) * stats[p, 1][:, :, :1])
    lane = lax.broadcasted_iota(jnp.int32, (dates, 1, LANES), 2)
    found = jnp.zeros((dates, 1, LANES), F32)
    for m in range(strips):
        here = corr[m]
        other = pltpu.roll(here.reshape(dates, LANES), WIN, 1).reshape(dates, 1, LANES)
        left = jnp.where(lane < WIN, here, other)
        right = jnp.where(lane < WIN, other, here)
        found = jnp.where(lane == 2 * m, left, jnp.where(lane == 2 * m + 1, right, found))
    sim_ref[p] = found.reshape(dates, LANES)[:, : sim_ref.shape[2]]


def interferogram(g, sizes, rgp_ref, ref32, shifted, pooled):
    dates, lines, strips = sizes
    rows = [pl.ds(g * (8 * LOOK_AZ) + k, 8, stride=LOOK_AZ) for k in range(LOOK_AZ)]
    sums = 0.0
    for base in range(0, strips, 2):
        terms = []
        for m in range(base, min(base + 2, strips)):
            rr = [ref32[0, m, at, :] for at in rows]
            ri = [ref32[1, m, at, :] for at in rows]
            column = []
            for d in range(dates):
                real = imag = 0.0
                for k, at in enumerate(rows):
                    sr = shifted[d, 0, m, at, :]
                    si = shifted[d, 1, m, at, :]
                    real = real + (rr[k] * sr + ri[k] * si)
                    imag = imag + (ri[k] * sr - rr[k] * si)
                column.append(jnp.concatenate([real, imag], axis=0))
            terms.append(split(jnp.concatenate(column, axis=0)))
        width = len(terms) * LANES
        lhs = jnp.concatenate(
            [jnp.concatenate([t[k] for t in terms], axis=1) for k in range(2)], axis=0
        )
        sums = sums + dot(lhs, rgp_ref[base * LANES : base * LANES + width])
    high = sums[: dates * 16]
    sums = high[:, :LANES] + (high[:, LANES:] + sums[dates * 16 :, :LANES])
    sums = sums.reshape(dates, 2, 8, LANES)
    sign = jnp.where(lax.broadcasted_iota(jnp.int32, (8, LANES), 1) < WIN, -1.0, 1.0)
    at = pl.ds(pl.multiple_of((g % (PATCH // 8)) * 8, 8), 8)
    for d in range(dates):
        pooled[d, at, :] = sums[d, 0] + turned(sums[d, 1], sign)


def goldstein(h, dates, out_ref, left_ref, right_ref, blk_ref, pooled):
    count = dates * PATCH
    sign = jnp.where(lax.broadcasted_iota(jnp.int32, (count, LANES), 1) < WIN, -1.0, 1.0)

    def down(x, sign):
        high, low = split(jnp.concatenate([x, turned(x, sign)], axis=0))
        both = dot(left_ref[0], jnp.concatenate([high, low], axis=1))
        return both[:, :LANES] + (both[:, LANES:] + dot(left_ref[1], high))

    spectrum = down(pooled[...].reshape(count, LANES), -sign)
    squares = spectrum * spectrum
    magnitude = root(squares + pltpu.roll(squares, WIN, 1))
    smooth = dot_right(magnitude, blk_ref[1]).reshape(-1, PATCH, LANES)
    smooth = (
        smooth
        + jnp.concatenate([smooth[:, 1:], smooth[:, :1]], axis=1)
        + jnp.concatenate([smooth[:, -1:], smooth[:, :-1]], axis=1)
    ).reshape(spectrum.shape)
    weighted = spectrum * root(smooth * (1.0 / 9.0))
    squares = weighted * weighted
    power = jnp.sum((squares + pltpu.roll(squares, WIN, 1)).reshape(-1, PATCH // 8, 8, LANES), axis=1)
    power = dot_right(power.reshape(-1, LANES), blk_ref[2]).reshape(-1, 8, LANES)
    scale = lax.rsqrt(jnp.sum(power, axis=1, keepdims=True) + RMS_EPS)
    high, low = split(down(weighted, sign))
    both = dot(high, right_ref[...])
    back = both[:, :LANES] + (both[:, LANES:] + dot(low, right_ref[:, :LANES]))
    scaled = back.reshape(-1, PATCH, LANES) * scale
    at = pl.ds(pl.multiple_of(h * PATCH, PATCH), PATCH)
    for d in range(dates):
        out_ref[d, 0, at, :] = scaled[d][:, :WIN]
        out_ref[d, 1, at, :] = scaled[d][:, WIN:]


def ring_device(position, count):
    half = count // 2
    return jnp.where(position < half, 2 * position, 2 * (count - 1 - position) + 1)


def kernel(
    at_hbm, ct_hbm, pr_hbm, img_ref, left_hbm, right_hbm, blk_hbm, rgp_hbm,
    sim_ref, out_ref, pooled,
    image, halo, ref, wide, shifted, devs, ref32, stats, root_stats,
    at_ref, ct_ref, pr_ref, left_ref, right_ref, blk_ref, rgp_ref,
    image_sem, root_sem, table_sem, halo_send, halo_recv, ref_send, ref_recv, dup_send,
):
    dates, _, lines, samples = img_ref.shape
    strips = samples // LANES
    rows = lines // WIN
    pieces = ref_send.shape[1]
    height = lines // pieces
    each = WIN // height
    groups = lines // (8 * LOOK_AZ)
    halves = lines // (LOOK_AZ * PATCH)
    sizes = (dates, lines, strips)
    count = lax.axis_size("date")
    az_count = lax.axis_size("az")
    az = lax.axis_index("az")
    mine = lax.axis_index("date")
    position = jnp.where(mine % 2 == 0, mine // 2, count - 1 - mine // 2)
    after = ring_device((position + 1) % count, count)
    before = ring_device((position + count - 1) % count, count)
    hops = (position, (count - position) % count)
    targets = (after, before)
    mesh_ids = pl.DeviceIdType.MESH

    def load(i):
        d = i // 2
        c = i % 2
        return pltpu.make_async_copy(img_ref.at[d, c], image.at[d, c], image_sem.at[i])

    for i in range(2 * dates):
        load(i).start()
    pairs = (
        (at_hbm, at_ref), (ct_hbm, ct_ref), (pr_hbm, pr_ref),
        (left_hbm, left_ref), (right_hbm, right_ref), (blk_hbm, blk_ref), (rgp_hbm, rgp_ref),
    )
    extras = [pltpu.make_async_copy(a, b, table_sem.at[i]) for i, (a, b) in enumerate(pairs)]
    for copy in extras:
        copy.start()
    own = pltpu.make_async_copy(img_ref.at[0], ref, root_sem)

    @pl.when(mine == 0)
    def _():
        own.start()

    barrier = pltpu.get_barrier_semaphore()
    for target in targets:
        pl.semaphore_signal(barrier, inc=1, device_id={"date": target}, device_id_type=mesh_ids)

    @pl.when(az > 0)
    def _():
        pl.semaphore_signal(barrier, inc=1, device_id={"az": az - 1}, device_id_type=mesh_ids)

    @pl.when(az < az_count - 1)
    def _():
        pl.semaphore_signal(barrier, inc=1, device_id={"az": az + 1}, device_id_type=mesh_ids)

    peers = 2 + jnp.where(az > 0, 1, 0) + jnp.where(az < az_count - 1, 1, 0)
    pl.semaphore_wait(barrier, peers)

    def relay(c, j, first):
        at = pl.ds(pl.multiple_of(j * height, height), height)
        return pltpu.make_async_remote_copy(
            src_ref=img_ref.at[0, c, at] if first else ref.at[c, at],
            dst_ref=ref.at[c, at],
            send_sem=ref_send.at[c, j],
            recv_sem=ref_recv.at[c, j],
            device_id={"date": targets[c]},
            device_id_type=mesh_ids,
        )

    dups = DUP if count > 2 else 0

    def direct(c, e):
        at = pl.ds(lines - (dups - e) * height, height)
        return pltpu.make_async_remote_copy(
            src_ref=img_ref.at[0, c, at],
            dst_ref=ref.at[c, at],
            send_sem=dup_send.at[c, e],
            recv_sem=ref_recv.at[c, pieces - dups + e],
            device_id={"date": targets[1 - c]},
            device_id_type=mesh_ids,
        )

    @pl.when(mine == 0)
    def _():
        def launch(j, carry):
            for c in range(2):
                relay(c, j, True).start()
            return carry

        lax.fori_loop(0, pieces, launch, 0)
        for e in range(dups):
            for c in range(2):
                direct(c, e).start()

    def sent(c):
        return jnp.where(hops[c] == count - 2, pieces - dups, jnp.where(hops[c] == count - 1, 0, pieces))

    def slot(t):
        for c in range(2):
            j = t - (hops[c] - 1) * LAG

            here = (hops[c] > 0) & (hops[c] < count - 1) & (j >= 0) & (j < pieces)

            @pl.when(here)
            def _():
                relay(c, j, False).wait_recv()

            @pl.when(here & (j < sent(c)))
            def _():
                relay(c, j, False).start()

    def edge(k):
        start = 0 if k else lines - MARGIN
        return pltpu.make_async_remote_copy(
            src_ref=img_ref.at[:, :, pl.ds(start, MARGIN)],
            dst_ref=halo.at[k],
            send_sem=halo_send.at[k],
            recv_sem=halo_recv.at[k],
            device_id={"az": az - 1 if k else az + 1},
            device_id_type=mesh_ids,
        )

    sends = (az < az_count - 1, az > 0)
    takes = (az > 0, az < az_count - 1)
    for k in range(2):
        @pl.when(sends[k])
        def _():
            edge(k).start()

    def widen(i, carry):
        d = i // 2
        c = i % 2
        load(i).wait()
        for m in range(strips):
            cols = slice(m * LANES, (m + 1) * LANES)
            wide[d, c, m, MARGIN : MARGIN + lines, :] = image[d, c, :, cols].astype(F32)
            wide[d, c, m, 2 * MARGIN + lines : 2 * MARGIN + lines + WIN, :] = jnp.zeros((WIN, LANES), F32)
        return carry

    lax.fori_loop(0, 2 * dates, widen, 0)
    slot(0)

    def fringe(k):
        first = MARGIN + lines if k else 0

        @pl.when(takes[k])
        def _():
            edge(k).wait_recv()

            def convert(i, carry):
                d = i // 2
                c = i % 2
                for m in range(strips):
                    cols = slice(m * LANES, (m + 1) * LANES)
                    wide[d, c, m, first : first + MARGIN, :] = halo[k, d, c, :, cols].astype(F32)
                return carry

            lax.fori_loop(0, 2 * dates, convert, 0)

        @pl.when(jnp.logical_not(takes[k]))
        def _():
            def clear(i, carry):
                for m in range(strips):
                    wide[i // 2, i % 2, m, first : first + MARGIN, :] = jnp.zeros((MARGIN, LANES), F32)
                return carry

            lax.fori_loop(0, 2 * dates, clear, 0)

    for copy in extras[:3]:
        copy.wait()

    def forward(t, carry):
        slot(t)
        return carry

    early_row = jnp.where(az % 2 == 0, rows - 1, 0)
    late_row = rows - 1 - early_row

    def outer(near):
        for k in range(2):
            @pl.when((az % 2 == 1 - k) == near)
            def _():
                fringe(k)

    def row_of(s):
        return jnp.where(s < rows - 2, s + 1, jnp.where(s == rows - 2, early_row, late_row))

    def shift(first, begin):
        def one(i, carry):
            @pl.when((i % PACE) == 0)
            def _():
                slot(first + i // PACE)

            @pl.when((begin == 0) & (i == dates * (rows - 2)))
            def _():
                outer(True)

            p = row_of(begin + i // dates)
            resample(p, i % dates, sizes, at_ref, ct_ref, pr_ref, wide, shifted, devs, stats)
            return carry

        return one

    inner = dates * (rows - 1)
    lax.fori_loop(0, inner, shift(1, 0), 0)
    for copy in extras[3:]:
        copy.wait()

    paced = 1 + -(-inner // PACE)

    def rest(s, carry):
        @pl.when(paced + s < HALO_SLOT)
        def _():
            slot(paced + s)

        settle(row_of(s), sizes, blk_ref, stats)
        return carry

    lax.fori_loop(0, rows - 1, rest, 0)
    lax.fori_loop(paced + rows - 1, HALO_SLOT, forward, 0)
    outer(False)
    lax.fori_loop(0, dates, shift(max(HALO_SLOT, paced), rows - 1), 0)
    settle(late_row, sizes, blk_ref, stats)

    @pl.when(mine == 0)
    def _():
        own.wait()

    begun = max(HALO_SLOT, paced) + -(-dates // PACE)
    last = pieces + max(0, count - 3) * LAG

    def due(j):
        ready = jnp.maximum(j + 1 + (count - 2) * LAG, begun + (j + 1) // 2)
        return jnp.where(j < 0, begun, jnp.minimum(last, ready))

    def take(j):
        lax.fori_loop(due(j - 1), due(j), forward, 0)
        for c in range(2):
            @pl.when(hops[c] == count - 1)
            def _():
                relay(c, j, False).wait_recv()

        prepare(j // each, j % each, height, sizes, ref, ref32, devs, stats, root_stats)

    def piece(j, carry):
        take(j)

        @pl.when(j % each == each - 1)
        def _():
            similarity(j // each, sizes, blk_ref, stats, root_stats, sim_ref)

        g = (j + 1) * height // (8 * LOOK_AZ) - 1

        @pl.when(g > j * height // (8 * LOOK_AZ) - 1)
        def _():
            interferogram(g, sizes, rgp_ref, ref32, shifted, pooled)

        h = (j + 1) * height // (LOOK_AZ * PATCH) - 1

        @pl.when(h > j * height // (LOOK_AZ * PATCH) - 1)
        def _():
            goldstein(h, dates, out_ref, left_ref, right_ref, blk_ref, pooled)

        return carry

    lax.fori_loop(0, pieces - 1, piece, 0)
    take(pieces - 1)
    similarity(rows - 1, sizes, blk_ref, stats, root_stats, sim_ref)
    interferogram(groups - 1, sizes, rgp_ref, ref32, shifted, pooled)

    for c in range(2):
        @pl.when(hops[c] < count - 1)
        def _():
            def drain(j, carry):
                relay(c, j, False).wait_send()
                return carry

            lax.fori_loop(0, sent(c), drain, 0)

    @pl.when(mine == 0)
    def _():
        for e in range(dups):
            for c in range(2):
                direct(c, e).wait_send()

    for k in range(2):
        @pl.when(sends[k])
        def _():
            edge(k).wait_send()


def finish(found_ref, early_ref, pooled_ref, left_ref, right_ref, blk_ref, sim_ref, out_ref):
    dates, _, early, _ = early_ref.shape
    sim_ref[...] = found_ref[...]
    out_ref[:, :, :early] = early_ref[...]
    goldstein(early // PATCH, dates, out_ref, left_ref, right_ref, blk_ref, pooled_ref)


def on_device(image, along, cross, present):
    dates, _, lines, samples = image.shape
    strips = samples // LANES
    rows = lines // WIN
    pieces = lines // PIECE
    halves = lines // (LOOK_AZ * PATCH)
    looks = samples // LOOK_RG
    vmem = pl.BlockSpec(memory_space=pltpu.VMEM)
    dma = pltpu.SemaphoreType.DMA
    left, right, blocks, rg_pool = tables(dates, samples)
    found, early, pooled = pl.pallas_call(
        kernel,
        out_shape=(
            jax.ShapeDtypeStruct((rows, dates, samples // WIN), F32),
            jax.ShapeDtypeStruct((dates, 2, (halves - 1) * PATCH, looks), F32),
            jax.ShapeDtypeStruct((dates, PATCH, 2 * looks), F32),
        ),
        in_specs=[pl.BlockSpec(memory_space=pl.ANY)] * 8,
        out_specs=(vmem, vmem, vmem),
        scratch_shapes=[
            pltpu.VMEM((dates, 2, lines, samples), BF16),
            pltpu.VMEM((2, dates, 2, MARGIN, samples), BF16),
            pltpu.VMEM((2, lines, samples), BF16),
            pltpu.VMEM((dates, 2, strips, lines + 2 * MARGIN + WIN, LANES), F32),
            pltpu.VMEM((dates, 2, strips, lines, LANES), F32),
            pltpu.VMEM((dates, strips, lines, LANES), F32),
            pltpu.VMEM((2, strips, lines, LANES), F32),
            pltpu.VMEM((rows, 3, strips, dates, 8, LANES), F32),
            pltpu.VMEM((rows, 3, strips, 8, LANES), F32),
            pltpu.SMEM((rows, dates, samples // WIN), jnp.int32),
            pltpu.SMEM((rows, dates, samples // WIN), jnp.int32),
            pltpu.SMEM((dates, rows), jnp.int32),
            pltpu.VMEM(left.shape, BF16),
            pltpu.VMEM(right.shape, BF16),
            pltpu.VMEM(blocks.shape, BF16),
            pltpu.VMEM(rg_pool.shape, BF16),
            dma((2 * dates,)),
            dma(()),
            dma((7,)),
            dma((2,)),
            dma((2,)),
            dma((2, pieces)),
            dma((2, pieces)),
            dma((2, DUP)),
        ],
        compiler_params=pltpu.CompilerParams(
            vmem_limit_bytes=62 * 1024 * 1024, collective_id=0, has_side_effects=True
        ),
    )(
        along.transpose(1, 0, 2), cross.transpose(1, 0, 2), present, image, left, right, blocks, rg_pool
    )
    found, filtered = pl.pallas_call(
        finish,
        out_shape=(
            jax.ShapeDtypeStruct(found.shape, F32),
            jax.ShapeDtypeStruct((dates, 2, lines // LOOK_AZ, looks), F32),
        ),
        in_specs=[vmem] * 6,
        out_specs=(vmem, vmem),
    )(found, early, pooled, left, right, blocks)
    return found.transpose(1, 0, 2), filtered


def solution(mesh):
    placed = (
        P("date", None, "az", None),
        P("date", "az", None),
        P("date", "az", None),
        P("date", "az"),
    )
    return jax.shard_map(
        on_device,
        mesh=mesh,
        in_specs=placed,
        out_specs=(P("date", "az", None), P("date", None, "az", None)),
        check_vma=False,
    )
```

```python
import jax
import jax.numpy as jnp
import ml_dtypes
import numpy as np
from jax import lax
from jax.experimental import pallas as pl
from jax.experimental.pallas import tpu as pltpu
from jax.sharding import PartitionSpec as P

WIN = 64
MARGIN = 32
LOOK_AZ = 5
LOOK_RG = 20
PATCH = 32
LANES = 128
PIECE = 16
LAG = 4
PACE = 2
HALO_SLOT = 12
BEHIND = 4
RATE = 2
FILTER = 12
MERGE = 2
DUP_EVEN = 4
DUP_ODD = 3

VAR_EPS = 1e-05
RMS_EPS = 1e-06
TINY = 1e-37

F32 = jnp.float32
BF16 = jnp.bfloat16


def two_terms(x):
    x = x.astype(np.float32)
    high = x.astype(ml_dtypes.bfloat16)
    return high, (x - high.astype(np.float32)).astype(ml_dtypes.bfloat16)


def tables(dates, samples):
    turns = np.outer(np.arange(PATCH), np.arange(PATCH)) % PATCH
    angles = turns * (2.0 * np.pi / PATCH)
    two = np.eye(samples // LOOK_RG // PATCH)
    cosine = np.kron(two, np.cos(angles))
    sine = np.kron(two, np.sin(angles))
    each = np.eye(dates)
    left = np.concatenate([np.kron(each, np.cos(angles)), np.kron(each, np.sin(angles))], axis=1)
    right = np.block([[cosine, sine], [-sine, cosine]])
    near = np.abs(np.arange(PATCH)[:, None] - np.arange(PATCH)[None, :])
    circular = np.minimum(near, PATCH - near) <= 1
    four = np.eye(LANES // PATCH)
    half = np.kron(np.eye(2), np.ones((WIN, WIN)))
    blocks = np.stack([half, np.kron(four, circular), np.kron(four, np.ones((PATCH, PATCH)))])
    blocks = np.concatenate([blocks, blocks], axis=1)
    pool = np.arange(samples)[:, None] // LOOK_RG == np.arange(samples // LOOK_RG)[None, :]
    pool = pool.astype(np.float64) @ np.concatenate([cosine, -sine], axis=1)
    return (
        jnp.asarray(np.stack(two_terms(left))),
        jnp.asarray(np.concatenate(two_terms(right), axis=1)),
        jnp.asarray(blocks, BF16),
        jnp.asarray(np.concatenate(two_terms(pool), axis=1)),
    )


def dot(a, b):
    return jnp.dot(a, b, preferred_element_type=F32)


def split(x):
    high = x.astype(BF16)
    return high, (x - high.astype(F32)).astype(BF16)


def dot_right(x, ones):
    return dot(jnp.concatenate(split(x), axis=1), ones)


def turned(x, sign):
    return sign * pltpu.roll(x, WIN, 1)


def root(x):
    return x * lax.rsqrt(jnp.maximum(x, TINY))


def resample(p, d, sizes, at_ref, ct_ref, pr_ref, wide, shifted, devs, stats):
    dates, lines, strips = sizes
    lane = lax.broadcasted_iota(jnp.int32, (WIN, LANES), 1)
    first = lane < WIN
    near_low = lane < LANES - MARGIN
    near_high = lane < MARGIN
    present = pr_ref[d, p]
    here = pl.ds(pl.multiple_of(p * WIN, WIN), WIN)
    for m in range(strips):
        rows = []
        turns = []
        for q in (2 * m, 2 * m + 1):
            start = jnp.where(
                present != 0, p * WIN + MARGIN + at_ref[p, d, q], lines + 2 * MARGIN
            )
            rows.append(pl.ds(start, WIN))
            turns.append((LANES - ct_ref[p, d, q]) & (LANES - 1))
        part = []
        for c in range(2):
            even = wide[d, c, m, rows[0], :]
            below = wide[d, c, m - 1, rows[0], :] if m > 0 else jnp.zeros_like(even)
            odd = wide[d, c, m, rows[1], :]
            above = wide[d, c, m + 1, rows[1], :] if m + 1 < strips else jnp.zeros_like(odd)
            even = pltpu.roll(jnp.where(near_low, even, below).astype(BF16), turns[0], 1)
            odd = pltpu.roll(jnp.where(near_high, above, odd).astype(BF16), turns[1], 1)
            part.append(jnp.where(first, even, odd).astype(F32))
            shifted[d, c, m, here, :] = part[c]
        amp = root(part[0] * part[0] + part[1] * part[1]).reshape(WIN // 8, 8, LANES)
        mean = jnp.sum(amp, axis=0) * (8.0 / WIN)
        dev = amp - mean[None]
        devs[d, m, here, :] = dev.reshape(WIN, LANES)
        stats[p, 0, m, d] = mean
        stats[p, 1, m, d] = jnp.sum(dev * dev, axis=0)


def total(x, half):
    sums = dot_right(x.reshape(-1, LANES), half).reshape(-1, 8, LANES)
    return jnp.sum(sums, axis=1, keepdims=True)


def settle(p, sizes, blk_ref, stats):
    dates, lines, strips = sizes
    half = blk_ref[0]
    shape = (strips * dates, 8, LANES)
    means = stats[p, 0].reshape(shape)
    away = means - total(means, half) * (1.0 / (8.0 * WIN))
    spread = stats[p, 1].reshape(shape) + (WIN / 8.0) * (away * away)
    var = total(spread, half) * (1.0 / (WIN * WIN))
    stats[p, 0] = away.reshape(strips, dates, 8, LANES)
    stats[p, 1] = jnp.broadcast_to(var + VAR_EPS, shape).reshape(strips, dates, 8, LANES)


def prepare(p, e, height, sizes, ref, ref32, devs, stats, own):
    dates, lines, strips = sizes
    here = pl.ds(pl.multiple_of(p * WIN + e * height, height), height)
    fresh = e == 0
    for m in range(strips):
        cols = slice(m * LANES, (m + 1) * LANES)
        real = ref[0, here, cols].astype(F32)
        imag = ref[1, here, cols].astype(F32)
        ref32[0, m, here, :] = real
        ref32[1, m, here, :] = imag
        amp = root(real * real + imag * imag).reshape(height // 8, 8, LANES)
        pivot = jnp.where(fresh, amp[0], own[p, 0, m])
        own[p, 0, m] = pivot
        dev = amp - pivot[None]
        own[p, 1, m] = jnp.sum(dev, axis=0) + jnp.where(fresh, 0.0, own[p, 1, m])
        own[p, 2, m] = jnp.sum(dev * dev, axis=0) + jnp.where(fresh, 0.0, own[p, 2, m])
        for d in range(dates):
            joint = devs[d, m, here, :].reshape(height // 8, 8, LANES) * dev
            stats[p, 2, m, d] = jnp.sum(joint, axis=0) + jnp.where(fresh, 0.0, stats[p, 2, m, d])


def similarity(p, sizes, blk_ref, stats, own, sim_ref):
    dates, lines, strips = sizes
    half = blk_ref[0]
    first = own[p, 1]
    means = own[p, 0] + first * (8.0 / WIN)
    away = means - total(means, half) * (1.0 / (8.0 * WIN))
    spread = own[p, 2] - first * first * (8.0 / WIN) + (WIN / 8.0) * (away * away)
    joint = stats[p, 2] + (WIN / 8.0) * (stats[p, 0] * away[:, None])
    every = jnp.concatenate([spread, joint.reshape(strips * dates, 8, LANES)], axis=0)
    every = total(every, half) * (1.0 / (WIN * WIN))
    var = every[:strips].reshape(strips, 1, 1, LANES)
    cov = every[strips:].reshape(strips, dates, 1, LANES)
    corr = cov * lax.rsqrt((var + VAR_EPS) * stats[p, 1][:, :, :1])
    lane = lax.broadcasted_iota(jnp.int32, (dates, 1, LANES), 2)
    found = jnp.zeros((dates, 1, LANES), F32)
    for m in range(strips):
        here = corr[m]
        other = pltpu.roll(here.reshape(dates, LANES), WIN, 1).reshape(dates, 1, LANES)
        left = jnp.where(lane < WIN, here, other)
        right = jnp.where(lane < WIN, other, here)
        found = jnp.where(lane == 2 * m, left, jnp.where(lane == 2 * m + 1, right, found))
    sim_ref[p] = found.reshape(dates, LANES)[:, : sim_ref.shape[2]]


def interferogram(g, sizes, rgp_ref, ref32, shifted, pooled):
    dates, lines, strips = sizes
    rows = [pl.ds(g * (8 * LOOK_AZ) + k, 8, stride=LOOK_AZ) for k in range(LOOK_AZ)]
    sums = 0.0
    for base in range(0, strips, 2):
        terms = []
        for m in range(base, min(base + 2, strips)):
            rr = [ref32[0, m, at, :] for at in rows]
            ri = [ref32[1, m, at, :] for at in rows]
            column = []
            for d in range(dates):
                real = imag = 0.0
                for k, at in enumerate(rows):
                    sr = shifted[d, 0, m, at, :]
                    si = shifted[d, 1, m, at, :]
                    real = real + (rr[k] * sr + ri[k] * si)
                    imag = imag + (ri[k] * sr - rr[k] * si)
                column.append(jnp.concatenate([real, imag], axis=0))
            terms.append(split(jnp.concatenate(column, axis=0)))
        width = len(terms) * LANES
        lhs = jnp.concatenate(
            [jnp.concatenate([t[k] for t in terms], axis=1) for k in range(2)], axis=0
        )
        sums = sums + dot(lhs, rgp_ref[base * LANES : base * LANES + width])
    high = sums[: dates * 16]
    sums = high[:, :LANES] + (high[:, LANES:] + sums[dates * 16 :, :LANES])
    sums = sums.reshape(dates, 2, 8, LANES)
    sign = jnp.where(lax.broadcasted_iota(jnp.int32, (8, LANES), 1) < WIN, -1.0, 1.0)
    at = pl.ds(pl.multiple_of((g % (PATCH // 8)) * 8, 8), 8)
    for d in range(dates):
        pooled[g // (PATCH // 8), d, at, :] = sums[d, 0] + turned(sums[d, 1], sign)


def goldstein(h, dates, out_ref, left_ref, right_ref, blk_ref, pooled):
    count = dates * PATCH
    sign = jnp.where(lax.broadcasted_iota(jnp.int32, (count, LANES), 1) < WIN, -1.0, 1.0)

    def down(x, sign):
        high, low = split(jnp.concatenate([x, turned(x, sign)], axis=0))
        both = dot(left_ref[0], jnp.concatenate([high, low], axis=1))
        return both[:, :LANES] + (both[:, LANES:] + dot(left_ref[1], high))

    spectrum = down(pooled[...].reshape(count, LANES), -sign)
    squares = spectrum * spectrum
    magnitude = root(squares + pltpu.roll(squares, WIN, 1))
    smooth = dot_right(magnitude, blk_ref[1]).reshape(-1, PATCH, LANES)
    smooth = (
        smooth
        + jnp.concatenate([smooth[:, 1:], smooth[:, :1]], axis=1)
        + jnp.concatenate([smooth[:, -1:], smooth[:, :-1]], axis=1)
    ).reshape(spectrum.shape)
    weighted = spectrum * root(smooth * (1.0 / 9.0))
    squares = weighted * weighted
    power = jnp.sum((squares + pltpu.roll(squares, WIN, 1)).reshape(-1, PATCH // 8, 8, LANES), axis=1)
    power = dot_right(power.reshape(-1, LANES), blk_ref[2]).reshape(-1, 8, LANES)
    scale = lax.rsqrt(jnp.sum(power, axis=1, keepdims=True) + RMS_EPS)
    high, low = split(down(weighted, sign))
    both = dot(high, right_ref[...])
    back = both[:, :LANES] + (both[:, LANES:] + dot(low, right_ref[:, :LANES]))
    scaled = back.reshape(-1, PATCH, LANES) * scale
    at = pl.ds(pl.multiple_of(h * PATCH, PATCH), PATCH)
    for d in range(dates):
        out_ref[d, 0, at, :] = scaled[d][:, :WIN]
        out_ref[d, 1, at, :] = scaled[d][:, WIN:]


def ring_device(position, count):
    half = count // 2
    return jnp.where(position < half, 2 * position, 2 * (count - 1 - position) + 1)


def kernel(
    at_hbm, ct_hbm, pr_hbm, img_ref, left_hbm, right_hbm, blk_hbm, rgp_hbm,
    sim_ref, out_ref, ending,
    image, halo, ref, wide, shifted, devs, ref32, stats, root_stats, pooled,
    at_ref, ct_ref, pr_ref, left_ref, right_ref, blk_ref, rgp_ref,
    image_sem, root_sem, table_sem, halo_send, halo_recv, ref_send, ref_recv, dup_send,
):
    dates, _, lines, samples = img_ref.shape
    strips = samples // LANES
    rows = lines // WIN
    pieces = ref_send.shape[1]
    height = lines // pieces
    each = WIN // height
    groups = lines // (8 * LOOK_AZ)
    halves = lines // (LOOK_AZ * PATCH)
    sizes = (dates, lines, strips)
    count = lax.axis_size("date")
    az_count = lax.axis_size("az")
    az = lax.axis_index("az")
    mine = lax.axis_index("date")
    position = jnp.where(mine % 2 == 0, mine // 2, count - 1 - mine // 2)
    after = ring_device((position + 1) % count, count)
    before = ring_device((position + count - 1) % count, count)
    hops = (position, (count - position) % count)
    targets = (after, before)
    mesh_ids = pl.DeviceIdType.MESH

    def load(i):
        d = i // 2
        c = i % 2
        return pltpu.make_async_copy(img_ref.at[d, c], image.at[d, c], image_sem.at[i])

    for i in range(2 * dates):
        load(i).start()
    pairs = (
        (at_hbm, at_ref), (ct_hbm, ct_ref), (pr_hbm, pr_ref),
        (left_hbm, left_ref), (right_hbm, right_ref), (blk_hbm, blk_ref), (rgp_hbm, rgp_ref),
    )
    extras = [pltpu.make_async_copy(a, b, table_sem.at[i]) for i, (a, b) in enumerate(pairs)]
    for copy in extras:
        copy.start()
    own = pltpu.make_async_copy(img_ref.at[0], ref, root_sem)

    @pl.when(mine == 0)
    def _():
        own.start()

    barrier = pltpu.get_barrier_semaphore()
    for target in targets:
        pl.semaphore_signal(barrier, inc=1, device_id={"date": target}, device_id_type=mesh_ids)

    @pl.when(az > 0)
    def _():
        pl.semaphore_signal(barrier, inc=1, device_id={"az": az - 1}, device_id_type=mesh_ids)

    @pl.when(az < az_count - 1)
    def _():
        pl.semaphore_signal(barrier, inc=1, device_id={"az": az + 1}, device_id_type=mesh_ids)

    peers = 2 + jnp.where(az > 0, 1, 0) + jnp.where(az < az_count - 1, 1, 0)
    pl.semaphore_wait(barrier, peers)

    def relay(c, j, first):
        at = pl.ds(pl.multiple_of(j * height, height), height)
        return pltpu.make_async_remote_copy(
            src_ref=img_ref.at[0, c, at] if first else ref.at[c, at],
            dst_ref=ref.at[c, at],
            send_sem=ref_send.at[c, j],
            recv_sem=ref_recv.at[c, j],
            device_id={"date": targets[c]},
            device_id_type=mesh_ids,
        )

    dups = jnp.where(az % 2 == 0, DUP_EVEN, DUP_ODD) if count > 2 else 0

    def direct(c, e):
        at = pl.ds(pl.multiple_of(lines - (dups - e) * height, height), height)
        return pltpu.make_async_remote_copy(
            src_ref=img_ref.at[0, c, at],
            dst_ref=ref.at[c, at],
            send_sem=dup_send.at[c, e],
            recv_sem=ref_recv.at[c, pieces - dups + e],
            device_id={"date": targets[1 - c]},
            device_id_type=mesh_ids,
        )

    @pl.when(mine == 0)
    def _():
        def launch(j, carry):
            for c in range(2):
                relay(c, j, True).start()
            return carry

        lax.fori_loop(0, pieces, launch, 0)

        def double(e, carry):
            for c in range(2):
                direct(c, e).start()
            return carry

        lax.fori_loop(0, dups, double, 0)

    def sent(c):
        return jnp.where(hops[c] == count - 2, pieces - dups, jnp.where(hops[c] == count - 1, 0, pieces))

    def slot(t):
        for c in range(2):
            j = t - (hops[c] - 1) * LAG

            here = (hops[c] > 0) & (hops[c] < count - 1) & (j >= 0) & (j < pieces)

            @pl.when(here)
            def _():
                relay(c, j, False).wait_recv()

            @pl.when(here & (j < sent(c)))
            def _():
                relay(c, j, False).start()

    def edge(k):
        start = 0 if k else lines - MARGIN
        return pltpu.make_async_remote_copy(
            src_ref=img_ref.at[:, :, pl.ds(start, MARGIN)],
            dst_ref=halo.at[k],
            send_sem=halo_send.at[k],
            recv_sem=halo_recv.at[k],
            device_id={"az": az - 1 if k else az + 1},
            device_id_type=mesh_ids,
        )

    sends = (az < az_count - 1, az > 0)
    takes = (az > 0, az < az_count - 1)
    for k in range(2):
        @pl.when(sends[k])
        def _():
            edge(k).start()

    def widen(i, carry):
        d = i // 2
        c = i % 2
        load(i).wait()
        for m in range(strips):
            cols = slice(m * LANES, (m + 1) * LANES)
            wide[d, c, m, MARGIN : MARGIN + lines, :] = image[d, c, :, cols].astype(F32)
            wide[d, c, m, 2 * MARGIN + lines : 2 * MARGIN + lines + WIN, :] = jnp.zeros((WIN, LANES), F32)
        return carry

    lax.fori_loop(0, 2 * dates, widen, 0)
    slot(0)

    def fringe(k):
        first = MARGIN + lines if k else 0

        @pl.when(takes[k])
        def _():
            edge(k).wait_recv()

            def convert(i, carry):
                d = i // 2
                c = i % 2
                for m in range(strips):
                    cols = slice(m * LANES, (m + 1) * LANES)
                    wide[d, c, m, first : first + MARGIN, :] = halo[k, d, c, :, cols].astype(F32)
                return carry

            lax.fori_loop(0, 2 * dates, convert, 0)

        @pl.when(jnp.logical_not(takes[k]))
        def _():
            def clear(i, carry):
                for m in range(strips):
                    wide[i // 2, i % 2, m, first : first + MARGIN, :] = jnp.zeros((MARGIN, LANES), F32)
                return carry

            lax.fori_loop(0, 2 * dates, clear, 0)

    for copy in extras[:3]:
        copy.wait()

    def forward(t, carry):
        slot(t)
        return carry

    early_row = jnp.where(az % 2 == 0, rows - 1, 0)
    late_row = rows - 1 - early_row

    def outer(near):
        for k in range(2):
            @pl.when((az % 2 == 1 - k) == near)
            def _():
                fringe(k)

    def row_of(s):
        return jnp.where(s < rows - 2, s + 1, jnp.where(s == rows - 2, early_row, late_row))

    def shift(first, begin):
        def one(i, carry):
            @pl.when((i % PACE) == 0)
            def _():
                slot(first + i // PACE)

            @pl.when((begin == 0) & (i == dates * (rows - 2)))
            def _():
                outer(True)

            p = row_of(begin + i // dates)
            resample(p, i % dates, sizes, at_ref, ct_ref, pr_ref, wide, shifted, devs, stats)
            return carry

        return one

    inner = dates * (rows - 1)
    lax.fori_loop(0, inner, shift(1, 0), 0)
    for copy in extras[3:]:
        copy.wait()

    paced = 1 + -(-inner // PACE)

    def rest(s, carry):
        @pl.when(paced + s < HALO_SLOT)
        def _():
            slot(paced + s)

        settle(row_of(s), sizes, blk_ref, stats)
        return carry

    lax.fori_loop(0, rows - 1, rest, 0)
    lax.fori_loop(paced + rows - 1, HALO_SLOT, forward, 0)
    outer(False)
    lax.fori_loop(0, dates, shift(max(HALO_SLOT, paced), rows - 1), 0)
    settle(late_row, sizes, blk_ref, stats)

    @pl.when(mine == 0)
    def _():
        own.wait()

    begun = max(HALO_SLOT, paced) + -(-dates // PACE)
    last = pieces + max(0, count - 3) * LAG

    behind = max((count - 2) * BEHIND, (count - 3) * LAG)

    def due(j):
        ready = jnp.maximum(j + 1 + behind, begun + (j + 1) // RATE)
        return jnp.where(j < 0, begun, jnp.minimum(last, ready))

    def take(j):
        lax.fori_loop(due(j - 1), due(j), forward, 0)
        for c in range(2):
            @pl.when(hops[c] == count - 1)
            def _():
                relay(c, j, False).wait_recv()

        prepare(j // each, j % each, height, sizes, ref, ref32, devs, stats, root_stats)

    def piece(j, carry):
        take(j)

        @pl.when((j >= each) & (j % each == MERGE))
        def _():
            similarity(j // each - 1, sizes, blk_ref, stats, root_stats, sim_ref)

        g = (j + 1) * height // (8 * LOOK_AZ) - 1

        @pl.when(g > j * height // (8 * LOOK_AZ) - 1)
        def _():
            interferogram(g, sizes, rgp_ref, ref32, shifted, pooled)

        for h in range(halves - 1):
            @pl.when(j == min(pieces - 2, h * (pieces // halves) + FILTER))
            def _():
                goldstein(h, dates, out_ref, left_ref, right_ref, blk_ref, pooled.at[h])

        return carry

    lax.fori_loop(0, pieces - 1, piece, 0)
    take(pieces - 1)
    similarity(rows - 1, sizes, blk_ref, stats, root_stats, sim_ref)
    interferogram(groups - 1, sizes, rgp_ref, ref32, shifted, pooled)
    ending[...] = pooled[halves - 1]

    for c in range(2):
        @pl.when(hops[c] < count - 1)
        def _():
            def drain(j, carry):
                relay(c, j, False).wait_send()
                return carry

            lax.fori_loop(0, sent(c), drain, 0)

    @pl.when(mine == 0)
    def _():
        def doubled(e, carry):
            for c in range(2):
                direct(c, e).wait_send()
            return carry

        lax.fori_loop(0, dups, doubled, 0)

    for k in range(2):
        @pl.when(sends[k])
        def _():
            edge(k).wait_send()


def finish(found_ref, early_ref, pooled_ref, left_ref, right_ref, blk_ref, sim_ref, out_ref):
    dates, _, early, _ = early_ref.shape
    sim_ref[...] = found_ref[...]
    out_ref[:, :, :early] = early_ref[...]
    goldstein(early // PATCH, dates, out_ref, left_ref, right_ref, blk_ref, pooled_ref)


def on_device(image, along, cross, present):
    dates, _, lines, samples = image.shape
    strips = samples // LANES
    rows = lines // WIN
    pieces = lines // PIECE
    halves = lines // (LOOK_AZ * PATCH)
    looks = samples // LOOK_RG
    vmem = pl.BlockSpec(memory_space=pltpu.VMEM)
    dma = pltpu.SemaphoreType.DMA
    left, right, blocks, rg_pool = tables(dates, samples)
    found, early, pooled = pl.pallas_call(
        kernel,
        out_shape=(
            jax.ShapeDtypeStruct((rows, dates, samples // WIN), F32),
            jax.ShapeDtypeStruct((dates, 2, (halves - 1) * PATCH, looks), F32),
            jax.ShapeDtypeStruct((dates, PATCH, 2 * looks), F32),
        ),
        in_specs=[pl.BlockSpec(memory_space=pl.ANY)] * 8,
        out_specs=(vmem, vmem, vmem),
        scratch_shapes=[
            pltpu.VMEM((dates, 2, lines, samples), BF16),
            pltpu.VMEM((2, dates, 2, MARGIN, samples), BF16),
            pltpu.VMEM((2, lines, samples), BF16),
            pltpu.VMEM((dates, 2, strips, lines + 2 * MARGIN + WIN, LANES), F32),
            pltpu.VMEM((dates, 2, strips, lines, LANES), F32),
            pltpu.VMEM((dates, strips, lines, LANES), F32),
            pltpu.VMEM((2, strips, lines, LANES), F32),
            pltpu.VMEM((rows, 3, strips, dates, 8, LANES), F32),
            pltpu.VMEM((rows, 3, strips, 8, LANES), F32),
            pltpu.VMEM((halves, dates, PATCH, 2 * looks), F32),
            pltpu.SMEM((rows, dates, samples // WIN), jnp.int32),
            pltpu.SMEM((rows, dates, samples // WIN), jnp.int32),
            pltpu.SMEM((dates, rows), jnp.int32),
            pltpu.VMEM(left.shape, BF16),
            pltpu.VMEM(right.shape, BF16),
            pltpu.VMEM(blocks.shape, BF16),
            pltpu.VMEM(rg_pool.shape, BF16),
            dma((2 * dates,)),
            dma(()),
            dma((7,)),
            dma((2,)),
            dma((2,)),
            dma((2, pieces)),
            dma((2, pieces)),
            dma((2, max(DUP_EVEN, DUP_ODD))),
        ],
        compiler_params=pltpu.CompilerParams(
            vmem_limit_bytes=62 * 1024 * 1024, collective_id=0, has_side_effects=True
        ),
    )(
        along.transpose(1, 0, 2), cross.transpose(1, 0, 2), present, image, left, right, blocks, rg_pool
    )
    found, filtered = pl.pallas_call(
        finish,
        out_shape=(
            jax.ShapeDtypeStruct(found.shape, F32),
            jax.ShapeDtypeStruct((dates, 2, lines // LOOK_AZ, looks), F32),
        ),
        in_specs=[vmem] * 6,
        out_specs=(vmem, vmem),
    )(found, early, pooled, left, right, blocks)
    return found.transpose(1, 0, 2), filtered


def solution(mesh):
    placed = (
        P("date", None, "az", None),
        P("date", "az", None),
        P("date", "az", None),
        P("date", "az"),
    )
    return jax.shard_map(
        on_device,
        mesh=mesh,
        in_specs=placed,
        out_specs=(P("date", "az", None), P("date", None, "az", None)),
        check_vma=False,
    )
```

```python
import jax
import jax.numpy as jnp
import ml_dtypes
import numpy as np
from jax import lax
from jax.experimental import pallas as pl
from jax.experimental.pallas import tpu as pltpu
from jax.sharding import PartitionSpec as P

WIN = 64
MARGIN = 32
LOOK_AZ = 5
LOOK_RG = 20
PATCH = 32
LANES = 128
PIECE = 16
LAG = 5
PACE = 2
HALO_SLOT = 12
BEHIND = 4
RATE = 2
FILTER = 12
MERGE = 2
DUP_EVEN = 4
DUP_ODD = 3

VAR_EPS = 1e-05
RMS_EPS = 1e-06
TINY = 1e-37

F32 = jnp.float32
BF16 = jnp.bfloat16


def two_terms(x):
    x = x.astype(np.float32)
    high = x.astype(ml_dtypes.bfloat16)
    return high, (x - high.astype(np.float32)).astype(ml_dtypes.bfloat16)


def tables(dates, samples):
    turns = np.outer(np.arange(PATCH), np.arange(PATCH)) % PATCH
    angles = turns * (2.0 * np.pi / PATCH)
    two = np.eye(samples // LOOK_RG // PATCH)
    cosine = np.kron(two, np.cos(angles))
    sine = np.kron(two, np.sin(angles))
    each = np.eye(dates)
    left = np.concatenate([np.kron(each, np.cos(angles)), np.kron(each, np.sin(angles))], axis=1)
    right = np.block([[cosine, sine], [-sine, cosine]])
    near = np.abs(np.arange(PATCH)[:, None] - np.arange(PATCH)[None, :])
    circular = np.minimum(near, PATCH - near) <= 1
    four = np.eye(LANES // PATCH)
    half = np.kron(np.eye(2), np.ones((WIN, WIN)))
    blocks = np.stack([half, np.kron(four, circular), np.kron(four, np.ones((PATCH, PATCH)))])
    blocks = np.concatenate([blocks, blocks], axis=1)
    pool = np.arange(samples)[:, None] // LOOK_RG == np.arange(samples // LOOK_RG)[None, :]
    pool = pool.astype(np.float64) @ np.concatenate([cosine, -sine], axis=1)
    return (
        jnp.asarray(np.stack(two_terms(left))),
        jnp.asarray(np.concatenate(two_terms(right), axis=1)),
        jnp.asarray(blocks, BF16),
        jnp.asarray(np.concatenate(two_terms(pool), axis=1)),
    )


def dot(a, b):
    return jnp.dot(a, b, preferred_element_type=F32)


def split(x):
    high = x.astype(BF16)
    return high, (x - high.astype(F32)).astype(BF16)


def dot_right(x, ones):
    return dot(jnp.concatenate(split(x), axis=1), ones)


def turned(x, sign):
    return sign * pltpu.roll(x, WIN, 1)


def root(x):
    return x * lax.rsqrt(jnp.maximum(x, TINY))


def resample(p, d, sizes, at_ref, ct_ref, pr_ref, wide, shifted, devs, stats):
    dates, lines, strips = sizes
    lane = lax.broadcasted_iota(jnp.int32, (WIN, LANES), 1)
    first = lane < WIN
    near_low = lane < LANES - MARGIN
    near_high = lane < MARGIN
    present = pr_ref[d, p]
    here = pl.ds(pl.multiple_of(p * WIN, WIN), WIN)
    for m in range(strips):
        rows = []
        turns = []
        for q in (2 * m, 2 * m + 1):
            start = jnp.where(
                present != 0, p * WIN + MARGIN + at_ref[p, d, q], lines + 2 * MARGIN
            )
            rows.append(pl.ds(start, WIN))
            turns.append((LANES - ct_ref[p, d, q]) & (LANES - 1))
        part = []
        for c in range(2):
            even = wide[d, c, m, rows[0], :]
            below = wide[d, c, m - 1, rows[0], :] if m > 0 else jnp.zeros_like(even)
            odd = wide[d, c, m, rows[1], :]
            above = wide[d, c, m + 1, rows[1], :] if m + 1 < strips else jnp.zeros_like(odd)
            even = pltpu.roll(jnp.where(near_low, even, below).astype(BF16), turns[0], 1)
            odd = pltpu.roll(jnp.where(near_high, above, odd).astype(BF16), turns[1], 1)
            part.append(jnp.where(first, even, odd).astype(F32))
            shifted[d, c, m, here, :] = part[c]
        amp = root(part[0] * part[0] + part[1] * part[1]).reshape(WIN // 8, 8, LANES)
        mean = jnp.sum(amp, axis=0) * (8.0 / WIN)
        dev = amp - mean[None]
        devs[d, m, here, :] = dev.reshape(WIN, LANES)
        stats[p, 0, m, d] = mean
        stats[p, 1, m, d] = jnp.sum(dev * dev, axis=0)


def total(x, half):
    sums = dot_right(x.reshape(-1, LANES), half).reshape(-1, 8, LANES)
    return jnp.sum(sums, axis=1, keepdims=True)


def settle(p, sizes, blk_ref, stats):
    dates, lines, strips = sizes
    half = blk_ref[0]
    shape = (strips * dates, 8, LANES)
    means = stats[p, 0].reshape(shape)
    away = means - total(means, half) * (1.0 / (8.0 * WIN))
    spread = stats[p, 1].reshape(shape) + (WIN / 8.0) * (away * away)
    var = total(spread, half) * (1.0 / (WIN * WIN))
    stats[p, 0] = away.reshape(strips, dates, 8, LANES)
    stats[p, 1] = jnp.broadcast_to(var + VAR_EPS, shape).reshape(strips, dates, 8, LANES)


def prepare(p, e, height, sizes, ref, ref32, devs, stats, own):
    dates, lines, strips = sizes
    here = pl.ds(pl.multiple_of(p * WIN + e * height, height), height)
    fresh = e == 0
    for m in range(strips):
        cols = slice(m * LANES, (m + 1) * LANES)
        real = ref[0, here, cols].astype(F32)
        imag = ref[1, here, cols].astype(F32)
        ref32[0, m, here, :] = real
        ref32[1, m, here, :] = imag
        amp = root(real * real + imag * imag).reshape(height // 8, 8, LANES)
        pivot = jnp.where(fresh, amp[0], own[p, 0, m])
        own[p, 0, m] = pivot
        dev = amp - pivot[None]
        own[p, 1, m] = jnp.sum(dev, axis=0) + jnp.where(fresh, 0.0, own[p, 1, m])
        own[p, 2, m] = jnp.sum(dev * dev, axis=0) + jnp.where(fresh, 0.0, own[p, 2, m])
        for d in range(dates):
            joint = devs[d, m, here, :].reshape(height // 8, 8, LANES) * dev
            stats[p, 2, m, d] = jnp.sum(joint, axis=0) + jnp.where(fresh, 0.0, stats[p, 2, m, d])


def similarity(p, sizes, blk_ref, stats, own, sim_ref):
    dates, lines, strips = sizes
    half = blk_ref[0]
    first = own[p, 1]
    means = own[p, 0] + first * (8.0 / WIN)
    away = means - total(means, half) * (1.0 / (8.0 * WIN))
    spread = own[p, 2] - first * first * (8.0 / WIN) + (WIN / 8.0) * (away * away)
    joint = stats[p, 2] + (WIN / 8.0) * (stats[p, 0] * away[:, None])
    every = jnp.concatenate([spread, joint.reshape(strips * dates, 8, LANES)], axis=0)
    every = total(every, half) * (1.0 / (WIN * WIN))
    var = every[:strips].reshape(strips, 1, 1, LANES)
    cov = every[strips:].reshape(strips, dates, 1, LANES)
    corr = cov * lax.rsqrt((var + VAR_EPS) * stats[p, 1][:, :, :1])
    lane = lax.broadcasted_iota(jnp.int32, (dates, 1, LANES), 2)
    found = jnp.zeros((dates, 1, LANES), F32)
    for m in range(strips):
        here = corr[m]
        other = pltpu.roll(here.reshape(dates, LANES), WIN, 1).reshape(dates, 1, LANES)
        left = jnp.where(lane < WIN, here, other)
        right = jnp.where(lane < WIN, other, here)
        found = jnp.where(lane == 2 * m, left, jnp.where(lane == 2 * m + 1, right, found))
    sim_ref[p] = found.reshape(dates, LANES)[:, : sim_ref.shape[2]]


def interferogram(g, sizes, rgp_ref, ref32, shifted, pooled):
    dates, lines, strips = sizes
    rows = [pl.ds(g * (8 * LOOK_AZ) + k, 8, stride=LOOK_AZ) for k in range(LOOK_AZ)]
    sums = 0.0
    for base in range(0, strips, 2):
        terms = []
        for m in range(base, min(base + 2, strips)):
            rr = [ref32[0, m, at, :] for at in rows]
            ri = [ref32[1, m, at, :] for at in rows]
            column = []
            for d in range(dates):
                real = imag = 0.0
                for k, at in enumerate(rows):
                    sr = shifted[d, 0, m, at, :]
                    si = shifted[d, 1, m, at, :]
                    real = real + (rr[k] * sr + ri[k] * si)
                    imag = imag + (ri[k] * sr - rr[k] * si)
                column.append(jnp.concatenate([real, imag], axis=0))
            terms.append(split(jnp.concatenate(column, axis=0)))
        width = len(terms) * LANES
        lhs = jnp.concatenate(
            [jnp.concatenate([t[k] for t in terms], axis=1) for k in range(2)], axis=0
        )
        sums = sums + dot(lhs, rgp_ref[base * LANES : base * LANES + width])
    high = sums[: dates * 16]
    sums = high[:, :LANES] + (high[:, LANES:] + sums[dates * 16 :, :LANES])
    sums = sums.reshape(dates, 2, 8, LANES)
    sign = jnp.where(lax.broadcasted_iota(jnp.int32, (8, LANES), 1) < WIN, -1.0, 1.0)
    at = pl.ds(pl.multiple_of((g % (PATCH // 8)) * 8, 8), 8)
    for d in range(dates):
        pooled[g // (PATCH // 8), d, at, :] = sums[d, 0] + turned(sums[d, 1], sign)


def goldstein(h, dates, out_ref, left_ref, right_ref, blk_ref, pooled):
    count = dates * PATCH
    sign = jnp.where(lax.broadcasted_iota(jnp.int32, (count, LANES), 1) < WIN, -1.0, 1.0)

    def down(x, sign):
        high, low = split(jnp.concatenate([x, turned(x, sign)], axis=0))
        both = dot(left_ref[0], jnp.concatenate([high, low], axis=1))
        return both[:, :LANES] + (both[:, LANES:] + dot(left_ref[1], high))

    spectrum = down(pooled[...].reshape(count, LANES), -sign)
    squares = spectrum * spectrum
    magnitude = root(squares + pltpu.roll(squares, WIN, 1))
    smooth = dot_right(magnitude, blk_ref[1]).reshape(-1, PATCH, LANES)
    smooth = (
        smooth
        + jnp.concatenate([smooth[:, 1:], smooth[:, :1]], axis=1)
        + jnp.concatenate([smooth[:, -1:], smooth[:, :-1]], axis=1)
    ).reshape(spectrum.shape)
    weighted = spectrum * root(smooth * (1.0 / 9.0))
    squares = weighted * weighted
    power = jnp.sum((squares + pltpu.roll(squares, WIN, 1)).reshape(-1, PATCH // 8, 8, LANES), axis=1)
    power = dot_right(power.reshape(-1, LANES), blk_ref[2]).reshape(-1, 8, LANES)
    scale = lax.rsqrt(jnp.sum(power, axis=1, keepdims=True) + RMS_EPS)
    high, low = split(down(weighted, sign))
    both = dot(high, right_ref[...])
    back = both[:, :LANES] + (both[:, LANES:] + dot(low, right_ref[:, :LANES]))
    scaled = back.reshape(-1, PATCH, LANES) * scale
    at = pl.ds(pl.multiple_of(h * PATCH, PATCH), PATCH)
    for d in range(dates):
        out_ref[d, 0, at, :] = scaled[d][:, :WIN]
        out_ref[d, 1, at, :] = scaled[d][:, WIN:]


def ring_device(position, count):
    half = count // 2
    return jnp.where(position < half, 2 * position, 2 * (count - 1 - position) + 1)


def kernel(
    at_hbm, ct_hbm, pr_hbm, img_ref, left_hbm, right_hbm, blk_hbm, rgp_hbm,
    sim_ref, out_ref, ending,
    image, halo, ref, wide, shifted, devs, ref32, stats, root_stats, pooled,
    at_ref, ct_ref, pr_ref, left_ref, right_ref, blk_ref, rgp_ref,
    image_sem, root_sem, table_sem, halo_send, halo_recv, ref_send, ref_recv, dup_send,
):
    dates, _, lines, samples = img_ref.shape
    strips = samples // LANES
    rows = lines // WIN
    pieces = ref_send.shape[1]
    height = lines // pieces
    each = WIN // height
    groups = lines // (8 * LOOK_AZ)
    halves = lines // (LOOK_AZ * PATCH)
    sizes = (dates, lines, strips)
    count = lax.axis_size("date")
    az_count = lax.axis_size("az")
    az = lax.axis_index("az")
    mine = lax.axis_index("date")
    position = jnp.where(mine % 2 == 0, mine // 2, count - 1 - mine // 2)
    after = ring_device((position + 1) % count, count)
    before = ring_device((position + count - 1) % count, count)
    hops = (position, (count - position) % count)
    targets = (after, before)
    mesh_ids = pl.DeviceIdType.MESH

    def load(i):
        d = i // 2
        c = i % 2
        return pltpu.make_async_copy(img_ref.at[d, c], image.at[d, c], image_sem.at[i])

    barrier = pltpu.get_barrier_semaphore()
    for target in targets:
        pl.semaphore_signal(barrier, inc=1, device_id={"date": target}, device_id_type=mesh_ids)

    @pl.when(az > 0)
    def _():
        pl.semaphore_signal(barrier, inc=1, device_id={"az": az - 1}, device_id_type=mesh_ids)

    @pl.when(az < az_count - 1)
    def _():
        pl.semaphore_signal(barrier, inc=1, device_id={"az": az + 1}, device_id_type=mesh_ids)

    for i in range(2 * dates):
        load(i).start()
    pairs = (
        (at_hbm, at_ref), (ct_hbm, ct_ref), (pr_hbm, pr_ref),
        (left_hbm, left_ref), (right_hbm, right_ref), (blk_hbm, blk_ref), (rgp_hbm, rgp_ref),
    )
    extras = [pltpu.make_async_copy(a, b, table_sem.at[i]) for i, (a, b) in enumerate(pairs)]
    for copy in extras:
        copy.start()
    own = pltpu.make_async_copy(img_ref.at[0], ref, root_sem)

    @pl.when(mine == 0)
    def _():
        own.start()

    peers = 2 + jnp.where(az > 0, 1, 0) + jnp.where(az < az_count - 1, 1, 0)
    pl.semaphore_wait(barrier, peers)

    def relay(c, j, first):
        at = pl.ds(pl.multiple_of(j * height, height), height)
        return pltpu.make_async_remote_copy(
            src_ref=img_ref.at[0, c, at] if first else ref.at[c, at],
            dst_ref=ref.at[c, at],
            send_sem=ref_send.at[c, j],
            recv_sem=ref_recv.at[c, j],
            device_id={"date": targets[c]},
            device_id_type=mesh_ids,
        )

    dups = jnp.where(az % 2 == 0, DUP_EVEN, DUP_ODD) if count > 2 else 0

    def direct(c, e):
        at = pl.ds(pl.multiple_of(lines - (dups - e) * height, height), height)
        return pltpu.make_async_remote_copy(
            src_ref=img_ref.at[0, c, at],
            dst_ref=ref.at[c, at],
            send_sem=dup_send.at[c, e],
            recv_sem=ref_recv.at[c, pieces - dups + e],
            device_id={"date": targets[1 - c]},
            device_id_type=mesh_ids,
        )

    @pl.when(mine == 0)
    def _():
        def launch(j, carry):
            for c in range(2):
                relay(c, j, True).start()
            return carry

        lax.fori_loop(0, pieces, launch, 0)

        def double(e, carry):
            for c in range(2):
                direct(c, e).start()
            return carry

        lax.fori_loop(0, dups, double, 0)

    def sent(c):
        return jnp.where(hops[c] == count - 2, pieces - dups, jnp.where(hops[c] == count - 1, 0, pieces))

    def slot(t):
        for c in range(2):
            j = t - (hops[c] - 1) * LAG

            here = (hops[c] > 0) & (hops[c] < count - 1) & (j >= 0) & (j < pieces)

            @pl.when(here)
            def _():
                relay(c, j, False).wait_recv()

            @pl.when(here & (j < sent(c)))
            def _():
                relay(c, j, False).start()

    def edge(k):
        start = 0 if k else lines - MARGIN
        return pltpu.make_async_remote_copy(
            src_ref=img_ref.at[:, :, pl.ds(start, MARGIN)],
            dst_ref=halo.at[k],
            send_sem=halo_send.at[k],
            recv_sem=halo_recv.at[k],
            device_id={"az": az - 1 if k else az + 1},
            device_id_type=mesh_ids,
        )

    sends = (az < az_count - 1, az > 0)
    takes = (az > 0, az < az_count - 1)
    for k in range(2):
        @pl.when(sends[k])
        def _():
            edge(k).start()

    def widen(i, carry):
        d = i // 2
        c = i % 2
        load(i).wait()
        for m in range(strips):
            cols = slice(m * LANES, (m + 1) * LANES)
            wide[d, c, m, MARGIN : MARGIN + lines, :] = image[d, c, :, cols].astype(F32)
            wide[d, c, m, 2 * MARGIN + lines : 2 * MARGIN + lines + WIN, :] = jnp.zeros((WIN, LANES), F32)
        return carry

    lax.fori_loop(0, 2 * dates, widen, 0)
    slot(0)

    def fringe(k):
        first = MARGIN + lines if k else 0

        @pl.when(takes[k])
        def _():
            edge(k).wait_recv()

            def convert(i, carry):
                d = i // 2
                c = i % 2
                for m in range(strips):
                    cols = slice(m * LANES, (m + 1) * LANES)
                    wide[d, c, m, first : first + MARGIN, :] = halo[k, d, c, :, cols].astype(F32)
                return carry

            lax.fori_loop(0, 2 * dates, convert, 0)

        @pl.when(jnp.logical_not(takes[k]))
        def _():
            def clear(i, carry):
                for m in range(strips):
                    wide[i // 2, i % 2, m, first : first + MARGIN, :] = jnp.zeros((MARGIN, LANES), F32)
                return carry

            lax.fori_loop(0, 2 * dates, clear, 0)

    for copy in extras[:3]:
        copy.wait()

    def forward(t, carry):
        slot(t)
        return carry

    early_row = jnp.where(az % 2 == 0, rows - 1, 0)
    late_row = rows - 1 - early_row

    def outer(near):
        for k in range(2):
            @pl.when((az % 2 == 1 - k) == near)
            def _():
                fringe(k)

    def row_of(s):
        return jnp.where(s < rows - 2, s + 1, jnp.where(s == rows - 2, early_row, late_row))

    def shift(first, begin):
        def one(i, carry):
            @pl.when((i % PACE) == 0)
            def _():
                slot(first + i // PACE)

            @pl.when((begin == 0) & (i == dates * (rows - 2)))
            def _():
                outer(True)

            p = row_of(begin + i // dates)
            resample(p, i % dates, sizes, at_ref, ct_ref, pr_ref, wide, shifted, devs, stats)
            return carry

        return one

    inner = dates * (rows - 1)
    lax.fori_loop(0, inner, shift(1, 0), 0)
    for copy in extras[3:]:
        copy.wait()

    paced = 1 + -(-inner // PACE)

    def rest(s, carry):
        @pl.when(paced + s < HALO_SLOT)
        def _():
            slot(paced + s)

        settle(row_of(s), sizes, blk_ref, stats)
        return carry

    lax.fori_loop(0, rows - 1, rest, 0)
    lax.fori_loop(paced + rows - 1, HALO_SLOT, forward, 0)
    outer(False)
    lax.fori_loop(0, dates, shift(max(HALO_SLOT, paced), rows - 1), 0)
    settle(late_row, sizes, blk_ref, stats)

    @pl.when(mine == 0)
    def _():
        own.wait()

    begun = max(HALO_SLOT, paced) + -(-dates // PACE)
    last = pieces + max(0, count - 3) * LAG

    behind = max((count - 2) * BEHIND, (count - 3) * LAG)

    def due(j):
        ready = jnp.maximum(j + 1 + behind, begun + (j + 1) // RATE)
        return jnp.where(j < 0, begun, jnp.minimum(last, ready))

    def take(j):
        lax.fori_loop(due(j - 1), due(j), forward, 0)
        for c in range(2):
            @pl.when(hops[c] == count - 1)
            def _():
                relay(c, j, False).wait_recv()

        prepare(j // each, j % each, height, sizes, ref, ref32, devs, stats, root_stats)

    def piece(j, carry):
        take(j)

        @pl.when((j >= each) & (j % each == MERGE))
        def _():
            similarity(j // each - 1, sizes, blk_ref, stats, root_stats, sim_ref)

        g = (j + 1) * height // (8 * LOOK_AZ) - 1

        @pl.when(g > j * height // (8 * LOOK_AZ) - 1)
        def _():
            interferogram(g, sizes, rgp_ref, ref32, shifted, pooled)

        for h in range(halves - 1):
            @pl.when(j == min(pieces - 2, h * (pieces // halves) + FILTER))
            def _():
                goldstein(h, dates, out_ref, left_ref, right_ref, blk_ref, pooled.at[h])

        return carry

    lax.fori_loop(0, pieces - 1, piece, 0)
    take(pieces - 1)
    similarity(rows - 1, sizes, blk_ref, stats, root_stats, sim_ref)
    interferogram(groups - 1, sizes, rgp_ref, ref32, shifted, pooled)
    ending[...] = pooled[halves - 1]

    for c in range(2):
        @pl.when(hops[c] < count - 1)
        def _():
            def drain(j, carry):
                relay(c, j, False).wait_send()
                return carry

            lax.fori_loop(0, sent(c), drain, 0)

    @pl.when(mine == 0)
    def _():
        def doubled(e, carry):
            for c in range(2):
                direct(c, e).wait_send()
            return carry

        lax.fori_loop(0, dups, doubled, 0)

    for k in range(2):
        @pl.when(sends[k])
        def _():
            edge(k).wait_send()


def finish(found_ref, early_ref, pooled_ref, left_ref, right_ref, blk_ref, sim_ref, out_ref):
    dates, _, early, _ = early_ref.shape
    sim_ref[...] = found_ref[...]
    out_ref[:, :, :early] = early_ref[...]
    goldstein(early // PATCH, dates, out_ref, left_ref, right_ref, blk_ref, pooled_ref)


def on_device(image, along, cross, present):
    dates, _, lines, samples = image.shape
    strips = samples // LANES
    rows = lines // WIN
    pieces = lines // PIECE
    halves = lines // (LOOK_AZ * PATCH)
    looks = samples // LOOK_RG
    vmem = pl.BlockSpec(memory_space=pltpu.VMEM)
    dma = pltpu.SemaphoreType.DMA
    left, right, blocks, rg_pool = tables(dates, samples)
    found, early, pooled = pl.pallas_call(
        kernel,
        out_shape=(
            jax.ShapeDtypeStruct((rows, dates, samples // WIN), F32),
            jax.ShapeDtypeStruct((dates, 2, (halves - 1) * PATCH, looks), F32),
            jax.ShapeDtypeStruct((dates, PATCH, 2 * looks), F32),
        ),
        in_specs=[pl.BlockSpec(memory_space=pl.ANY)] * 8,
        out_specs=(vmem, vmem, vmem),
        scratch_shapes=[
            pltpu.VMEM((dates, 2, lines, samples), BF16),
            pltpu.VMEM((2, dates, 2, MARGIN, samples), BF16),
            pltpu.VMEM((2, lines, samples), BF16),
            pltpu.VMEM((dates, 2, strips, lines + 2 * MARGIN + WIN, LANES), F32),
            pltpu.VMEM((dates, 2, strips, lines, LANES), F32),
            pltpu.VMEM((dates, strips, lines, LANES), F32),
            pltpu.VMEM((2, strips, lines, LANES), F32),
            pltpu.VMEM((rows, 3, strips, dates, 8, LANES), F32),
            pltpu.VMEM((rows, 3, strips, 8, LANES), F32),
            pltpu.VMEM((halves, dates, PATCH, 2 * looks), F32),
            pltpu.SMEM((rows, dates, samples // WIN), jnp.int32),
            pltpu.SMEM((rows, dates, samples // WIN), jnp.int32),
            pltpu.SMEM((dates, rows), jnp.int32),
            pltpu.VMEM(left.shape, BF16),
            pltpu.VMEM(right.shape, BF16),
            pltpu.VMEM(blocks.shape, BF16),
            pltpu.VMEM(rg_pool.shape, BF16),
            dma((2 * dates,)),
            dma(()),
            dma((7,)),
            dma((2,)),
            dma((2,)),
            dma((2, pieces)),
            dma((2, pieces)),
            dma((2, max(DUP_EVEN, DUP_ODD))),
        ],
        compiler_params=pltpu.CompilerParams(
            vmem_limit_bytes=62 * 1024 * 1024, collective_id=0, has_side_effects=True
        ),
    )(
        along.transpose(1, 0, 2), cross.transpose(1, 0, 2), present, image, left, right, blocks, rg_pool
    )
    found, filtered = pl.pallas_call(
        finish,
        out_shape=(
            jax.ShapeDtypeStruct(found.shape, F32),
            jax.ShapeDtypeStruct((dates, 2, lines // LOOK_AZ, looks), F32),
        ),
        in_specs=[vmem] * 6,
        out_specs=(vmem, vmem),
    )(found, early, pooled, left, right, blocks)
    return found.transpose(1, 0, 2), filtered


def solution(mesh):
    placed = (
        P("date", None, "az", None),
        P("date", "az", None),
        P("date", "az", None),
        P("date", "az"),
    )
    return jax.shard_map(
        on_device,
        mesh=mesh,
        in_specs=placed,
        out_specs=(P("date", "az", None), P("date", None, "az", None)),
        check_vma=False,
    )
```
